32 devices in a mesh: dp: 4 (over y, core), mp: 8 (over z, x).
Axes of the slice: x: 2, y: 2, z: 4, core: 2. Of those that a mesh axis runs over, the one named last changes fastest.
Arguments:
- layer_input: bfloat16 [2048, 4096], P('dp', 'mp'), may hold values from -6 to 6
- gate_pre: bfloat16 [2048, 14336], P('dp', 'mp'), may hold values from -6 to 6
- up_pre: bfloat16 [2048, 14336], P('dp', 'mp'), may hold values from -6 to 6
- out_grad: bfloat16 [2048, 4096], P('dp', 'mp'), may hold values from -36 to 36
- w_down: bfloat16 [14336, 4096], P('mp'), may hold values from -0.09375 to 0.09375
- proj_input: bfloat16 [4096, 64], P('mp'), may hold values from -4 to 4
- proj_hidden: bfloat16 [14336, 64], P('mp'), may hold values from -4 to 4
- proj_gate: bfloat16 [14336, 64], P('mp'), may hold values from -0.046875 to 0.046875
- proj_upward: bfloat16 [14336, 64], P('mp'), may hold values from -0.046875 to 0.046875
- proj_output: bfloat16 [64, 4096], P(None, 'mp'), may hold values from -0.09375 to 0.09375
- seq_ids: int32 [4, 512], P('dp'), may hold values from 0 to 7, never falling along the last dimension, each value on 1 to 128 neighbouring positions
Outputs:
- features: float32 [32, 3, 4096], P('dp', None, 'mp')
The draws below stay inside these ranges and needn't reach their ends.
Inputs may be any that keep to these rules, and one draw needn't show every extreme that they name: `seq_ids`: within each row the ids never fall and every id appears; every sequence has 1 to 128 tokens and some sequence of each row has exactly 128.
All inputs are finite; a program needn't handle non-finite values.
Results may differ from the reference program's by a relative error of at most 0.0029.
Values may be sent and summed in bfloat16 or wider, within the bound.
A program may use at most 64 MiB of HBM per device.

```python
import math
import jax
import jax.numpy as jnp
import numpy as np
from jax import lax

D = 4096
FF = 14336
RANK = 64
SEQ_LEN = 64
TOK_DEV = 512
SEQ_DEV = 8
LMAX = 128
GROUPS = 4
TOKENS = 2048
SEQS = 32


def column_projection(key, fan_rows, low_scale, high_scale):
    first_key, second_key = jax.random.split(key)
    base = jnp.clip(jax.random.normal(first_key, (fan_rows, RANK), jnp.float32), -4.0, 4.0)
    rising = jnp.sqrt(1.0 + 2.0 * jnp.arange(RANK, dtype=jnp.float32) / (RANK - 1))
    spread = jnp.exp(jax.random.uniform(second_key, (RANK,), jnp.float32, math.log(low_scale), math.log(high_scale)))
    return (base * (rising * spread)[None, :] / math.sqrt(fan_rows)).astype(jnp.bfloat16)


def draw_proj_input(key, part):
    key = jax.random.fold_in(key, 21)
    return column_projection(key, D, 0.3, 3.0)


def draw_proj_hidden(key, part):
    key = jax.random.fold_in(key, 31)
    return column_projection(key, FF, 0.3, 3.0)


def draw_out_grad(key, part):
    key = jax.random.fold_in(key, 11)
    first_key, second_key = jax.random.split(key, 2)
    blocks = TOKENS // SEQ_LEN
    spread = jnp.exp(jax.random.uniform(second_key, (blocks,), jnp.float32, 0.0, math.log(10.0)))
    base = jnp.clip(jax.random.normal(first_key, (TOKENS, D), jnp.float32), -4.0, 4.0)
    positions = jnp.arange(TOKENS, dtype=jnp.int32)
    rising = 1.0 + 2.0 * positions.astype(jnp.float32) / (TOKENS - 1)
    row_scale = 0.3 * rising * spread[positions // SEQ_LEN]
    return (base * row_scale[:, None]).astype(jnp.bfloat16)


def steps_of(stream_key, extent, cuts, smallest, high):
    gain, own = 1.0, jax.random.fold_in(stream_key, 6)
    for position, blocks in cuts:
        steps = jnp.exp(jax.random.uniform(jax.random.fold_in(own, position), (blocks,), jnp.float32, smallest / len(cuts), high / len(cuts)))
        gain = gain * jnp.repeat(steps, extent[position] // blocks).reshape([-1 if axis == position else 1 for axis in range(len(extent))])
    return gain


def split_up(amount, total, bound, skew):
    loads = [(1 << 20) // math.isqrt(standing ** skew) + 1 for standing in range(2, amount + 1)]
    spare, holding = total - bound - (amount - 1), [1] * (amount - 1)
    while spare > 0:
        candidates = [i for i in range(amount - 1) if holding[i] < bound]
        whole, remaining = sum([loads[i] for i in candidates]), spare
        for i in candidates:
            more = min(bound - holding[i], max(1, remaining * loads[i] // whole), spare)
            holding[i] = holding[i] + more
            spare = spare - more
    return np.array([bound] + holding)


def ragged(rng, count, total, bound, lean):
    if count == 2:
        one = jax.random.randint(rng, (), max(1, total - bound), min(bound, total - 1) + 1)
        return jnp.stack([one, total - one])
    lengths = jnp.asarray(split_up(count, total, bound, lean), jnp.int32)
    couples = (count - 1) // 2
    donor, sink = lengths[1:1 + 2 * couples:2], lengths[2:2 + 2 * couples:2]
    slack = jnp.minimum(donor - 1, bound - sink)
    passed = jax.random.randint(jax.random.fold_in(rng, 1), (couples,), 0, 1 << 20) % (slack + 1)
    lengths = lengths.at[1:1 + 2 * couples:2].set(donor - passed).at[2:2 + 2 * couples:2].set(sink + passed)
    return lengths[jax.random.permutation(jax.random.fold_in(rng, 2), count)]


def bell_draw(own_key, extent, scale, bound, pieces=(), kind=jnp.bfloat16):
    entries = scale * jax.random.normal(own_key, extent, jnp.float32)
    if pieces:
        entries = entries * steps_of(own_key, extent, pieces, -0.22, 0.18)
    return jnp.clip(entries, -bound, bound).astype(kind)


def setup_inputs(seed: int = 0) -> dict:
    keys = jax.random.split(jax.random.key(seed), 12)
    layer_input = bell_draw(keys[0], (TOKENS, D), 1.0, 6.0, ((0, 4), (1, 8)))
    gate_pre = bell_draw(keys[1], (TOKENS, FF), 1.0, 6.0, ((0, 4), (1, 8)))
    up_pre = bell_draw(keys[2], (TOKENS, FF), 1.0, 6.0, ((0, 4), (1, 8)))
    out_grad = draw_out_grad(jax.random.fold_in(keys[11], 71), 0)
    w_down = bell_draw(keys[4], (FF, D), D ** -0.5, 0.09375, ((0, 8),))
    proj_input = draw_proj_input(jax.random.fold_in(keys[11], 71), 0)
    proj_hidden = draw_proj_hidden(jax.random.fold_in(keys[11], 71), 0)
    proj_gate = bell_draw(keys[7], (FF, RANK), FF ** -0.5, 0.046875, ((0, 8),))
    proj_upward = bell_draw(keys[8], (FF, RANK), FF ** -0.5, 0.046875, ((0, 8),))
    proj_output = bell_draw(keys[9], (RANK, D), D ** -0.5, 0.09375, ((1, 8),))
    seq_ids = jax.vmap(lambda own: jnp.searchsorted(jnp.cumsum(ragged(own, SEQ_DEV, TOK_DEV, LMAX, 1)), jnp.arange(TOK_DEV), side="right"))(jax.random.split(keys[10], GROUPS)).reshape((GROUPS, TOK_DEV)).astype(jnp.int32)
    return {"layer_input": layer_input, "gate_pre": gate_pre, "up_pre": up_pre, "out_grad": out_grad, "w_down": w_down, "proj_input": proj_input, "proj_hidden": proj_hidden, "proj_gate": proj_gate, "proj_upward": proj_upward, "proj_output": proj_output, "seq_ids": seq_ids}


def silu_parts(gate_value):
    sigmoid_v = jax.nn.sigmoid(gate_value)
    return (gate_value * sigmoid_v, sigmoid_v * (1.0 + gate_value * (1.0 - sigmoid_v)))

def outer_sum(member, left_side, right_side):
    weighted = member[:, :, None] * left_side[None, :, :]
    joined = jnp.einsum('sti,tj->sij', weighted, right_side, precision=lax.Precision.HIGHEST)
    return joined.reshape(member.shape[0], -1)

def reference(layer_input, gate_pre, up_pre, out_grad, w_down, proj_input, proj_hidden, proj_gate, proj_upward, proj_output, seq_ids):
    contract = (((1,), (1,)), ((), ()))

    def one_group(blocks):
        group_input, group_gate, group_up, group_grad, seq_row = blocks
        gate_value = group_gate.astype(jnp.float32)
        up_value = group_up.astype(jnp.float32)
        activated, slope_value = silu_parts(gate_value)
        hidden = (activated * up_value).astype(jnp.bfloat16)
        hidden_grad = lax.dot_general(group_grad, w_down, contract, preferred_element_type=jnp.float32)
        gate_grad = (hidden_grad * up_value * slope_value).astype(jnp.bfloat16)
        upward_grad = (hidden_grad * activated).astype(jnp.bfloat16)
        in_factor = jnp.dot(group_input, proj_input, preferred_element_type=jnp.float32)
        hid_factor = jnp.dot(hidden, proj_hidden, preferred_element_type=jnp.float32)
        gate_factor = jnp.dot(gate_grad, proj_gate, preferred_element_type=jnp.float32)
        up_factor = jnp.dot(upward_grad, proj_upward, preferred_element_type=jnp.float32)
        out_factor = lax.dot_general(group_grad, proj_output, contract, preferred_element_type=jnp.float32)
        member = (seq_row[None, :] == jnp.arange(SEQ_DEV, dtype=jnp.int32)[:, None]).astype(jnp.float32)
        return jnp.stack([outer_sum(member, in_factor, gate_factor), outer_sum(member, in_factor, up_factor), outer_sum(member, hid_factor, out_factor)], axis=1)
    raw_feat = lax.map(one_group, (layer_input.reshape(GROUPS, TOK_DEV, D), gate_pre.reshape(GROUPS, TOK_DEV, FF), up_pre.reshape(GROUPS, TOK_DEV, FF), out_grad.reshape(GROUPS, TOK_DEV, D), seq_ids))
    raw_feat = raw_feat.reshape(SEQS, 3, RANK * RANK)
    scale_value = lax.rsqrt(lax.optimization_barrier(jnp.mean(raw_feat * raw_feat, axis=(0, 2))) + 1e-06)
    return raw_feat * scale_value[None, :, None]
```

```python
import functools

import jax
import jax.numpy as jnp
from jax import lax
from jax.experimental import pallas as pl
from jax.experimental.pallas import tpu as pltpu
from jax.sharding import PartitionSpec as P

SEQ_DEV = 8


def silu_parts(gate_value):
    sigmoid_v = jax.nn.sigmoid(gate_value)
    return (gate_value * sigmoid_v, sigmoid_v * (1.0 + gate_value * (1.0 - sigmoid_v)))


def layer_features(member, left_in, left_hid, gate_factor, up_factor, out_factor):
    seq_count = member.shape[0]
    tok_rows = member.shape[1]
    left_width = left_in.shape[1]
    rank_dim = out_factor.shape[1]
    weighted_in = (member[:, None, :] * left_in.T[None, :, :]).reshape(
        seq_count * left_width, tok_rows
    )
    weighted_hid = (member[:, None, :] * left_hid.T[None, :, :]).reshape(
        seq_count * left_width, tok_rows
    )
    paired = jnp.dot(
        weighted_in,
        jnp.concatenate([gate_factor, up_factor], axis=1),
        precision=lax.Precision.HIGHEST,
    )
    paired = paired.reshape(seq_count, left_width, 2, rank_dim)
    gate_feat = paired[:, :, 0, :].reshape(seq_count, left_width * rank_dim)
    up_feat = paired[:, :, 1, :].reshape(seq_count, left_width * rank_dim)
    down_feat = jnp.dot(weighted_hid, out_factor, precision=lax.Precision.HIGHEST).reshape(
        seq_count, left_width * rank_dim
    )
    return jnp.stack([gate_feat, up_feat, down_feat], axis=1)


def per_device(
    layer_input,
    gate_pre,
    up_pre,
    out_grad,
    w_down,
    proj_input,
    proj_hidden,
    proj_gate,
    proj_upward,
    proj_output,
    seq_ids,
):
    contract = (((1,), (1,)), ((), ()))
    rank_dim = proj_input.shape[1]
    own_width = rank_dim // lax.axis_size("mp")
    position = lax.axis_index("mp")
    gate_value = gate_pre.astype(jnp.float32)
    up_value = up_pre.astype(jnp.float32)
    activated, slope_value = silu_parts(gate_value)
    hidden = (activated * up_value).astype(jnp.bfloat16)
    in_part = jnp.dot(layer_input, proj_input, preferred_element_type=jnp.float32)
    hid_part = jnp.dot(hidden, proj_hidden, preferred_element_type=jnp.float32)
    hidden_grad = lax.dot_general(
        lax.all_gather(out_grad, "mp", axis=1, tiled=True),
        w_down,
        contract,
        preferred_element_type=jnp.float32,
    )
    out_part = lax.dot_general(out_grad, proj_output, contract, preferred_element_type=jnp.float32)
    gate_grad = (hidden_grad * up_value * slope_value).astype(jnp.bfloat16)
    upward_grad = (hidden_grad * activated).astype(jnp.bfloat16)
    gate_part = jnp.dot(gate_grad, proj_gate, preferred_element_type=jnp.float32)
    up_part = jnp.dot(upward_grad, proj_upward, preferred_element_type=jnp.float32)
    gate_part, up_part = (gate_part, up_part)
    in_factor, hid_factor, gate_factor, up_factor, out_factor = lax.psum(
        (in_part, hid_part, gate_part, up_part, out_part), "mp"
    )
    member = (seq_ids[0][None, :] == jnp.arange(SEQ_DEV, dtype=jnp.int32)[:, None]).astype(
        jnp.float32
    )
    own_in = lax.dynamic_slice_in_dim(in_factor, position * own_width, own_width, 1)
    own_hid = lax.dynamic_slice_in_dim(hid_factor, position * own_width, own_width, 1)
    raw_feat = layer_features(member, own_in, own_hid, gate_factor, up_factor, out_factor)
    squares = jnp.sum(raw_feat * raw_feat, axis=(0, 2))
    total_sq = lax.psum(squares, ("dp", "mp"))
    entries = raw_feat.shape[0] * lax.axis_size("dp") * rank_dim * rank_dim
    scale_value = lax.rsqrt(total_sq / entries + 1e-06)
    return raw_feat * scale_value[None, :, None]


MESH = pl.DeviceIdType.MESH
ROWS_Z, COLS_X = 4, 2
PIECES = 4
X_FIRST = 0
TILE = 256
ROWS = 128
NT = (((1,), (1,)), ((), ()))
UP, DOWN, ACROSS = 0, 1, 2


def fused_kernel(
    ndp, nmp,
    x_hbm, gate_hbm, up_hbm, grad_hbm, w_hbm, pin_hbm, phid_hbm, pgate_hbm, pup_hbm, pout_hbm, seq_hbm,
    out_ref,
    x_v, gate_v, up_v, grad_v, w_v, pin_v, phid_v, pgate_v, pup_v, pout_v, seq_v,
    hgrad, act, upslope, hid_tile, up_tile, acc_a, acc_b,
    fac_send, fac_recv, full, weighted, raw_own, raw_send, raw_recv,
    sq_mine, sq_recv, sq_group, sq_dp,
    load_sem, w_sem, g_send, g_recv, fac_ss, fac_rs, full_ss, full_rs, raw_ss, raw_rs,
    sq_ss, sq_rs, dp_ss, dp_rs,
):
    dp = lax.axis_index("dp")
    me = lax.axis_index("mp")
    z, x = me // COLS_X, lax.rem(me, COLS_X)
    xo = 1 - x
    tokens, width = grad_hbm.shape
    tiles = w_hbm.shape[0] // TILE
    rank = pin_hbm.shape[1]
    own = rank // nmp
    prow = tokens // PIECES
    f32, bf16 = jnp.float32, jnp.bfloat16

    def at(zz, xx):
        return zz * COLS_X + xx

    loads = [
        pltpu.make_async_copy(src, dst, load_sem.at[i])
        for i, (src, dst) in enumerate(
            [
                (grad_hbm, grad_v.at[me]), (x_hbm, x_v), (pin_hbm, pin_v), (pout_hbm, pout_v), (seq_hbm, seq_v),
                (gate_hbm, gate_v), (up_hbm, up_v), (phid_hbm, phid_v), (pgate_hbm, pgate_v), (pup_hbm, pup_v),
            ]
        )
    ]
    for load in loads:
        load.start()
    w_loads = [
        pltpu.make_async_copy(w_hbm.at[:, pl.ds(b * width, width)], w_v.at[b], w_sem.at[b]) for b in range(nmp)
    ]
    for load in w_loads:
        load.start()

    barrier = pltpu.get_barrier_semaphore()
    mp_peers = [lax.rem(me + k, nmp) for k in range(1, nmp)]
    dp_peers = [lax.rem(dp + k, ndp) for k in range(1, ndp)]
    for peer in mp_peers:
        pl.semaphore_signal(barrier, inc=1, device_id=(dp, peer), device_id_type=MESH)
    for peer in dp_peers:
        pl.semaphore_signal(barrier, inc=1, device_id=(peer, me), device_id_type=MESH)
    loads[0].wait()
    pl.semaphore_wait(barrier, len(mp_peers) + len(dp_peers))

    def piece(kind, block, c, target):
        ref = grad_v.at[block, pl.ds(pl.multiple_of(c * prow, prow), prow), :]
        return pltpu.make_async_remote_copy(
            src_ref=ref, dst_ref=ref, send_sem=g_send.at[kind, block, c], recv_sem=g_recv.at[block, c],
            device_id=(dp, target), device_id_type=MESH,
        )

    def arrived(block, c):
        piece(ACROSS, block, c, at(z, xo)).wait_recv()

    def upward(block, c, op):
        @pl.when(z < ROWS_Z - 1)
        def _():
            op(piece(UP, block, c, at(z + 1, x)))

    def downward(block, c, op):
        @pl.when(z > 0)
        def _():
            op(piece(DOWN, block, c, at(z - 1, x)))

    def across(block, c, op):
        op(piece(ACROSS, block, c, at(z, xo)))

    def start(copy):
        copy.start()

    def done(copy):
        copy.wait_send()

    def own_block(op):
        @pl.loop(0, PIECES)
        def _(c):
            across(me, c, op)
            upward(me, c, op)
            downward(me, c, op)

    def same_column(level, op, wait):
        @pl.loop(0, PIECES)
        def _(c):
            for sign, onward in ((1, downward), (-1, upward)):
                far = z + sign * level

                @pl.when((far >= 0) & (far < ROWS_Z))
                def _():
                    block = at(far, x)
                    if wait:
                        arrived(block, c)
                    onward(block, c, op)
                    if X_FIRST == 0:
                        across(block, c, op)
                    elif X_FIRST < PIECES:
                        @pl.when(c >= X_FIRST)
                        def _():
                            across(block, c, op)

    def crossed(dist, op, wait):
        if X_FIRST == 0:
            return

        @pl.loop(0, X_FIRST)
        def _(c):
            if dist == 0:
                block = at(z, xo)
                if wait:
                    arrived(block, c)
                upward(block, c, op)
                downward(block, c, op)
                return
            for sign, onward in ((1, downward), (-1, upward)):
                far = z + sign * dist

                @pl.when((far >= 0) & (far < ROWS_Z))
                def _():
                    block = at(far, xo)
                    if wait:
                        arrived(block, c)
                    onward(block, c, op)

    def rest_of(block):
        @pl.loop(X_FIRST, PIECES)
        def _(c):
            arrived(block, c)

    def add_block(block, first=False):
        @pl.loop(0, tiles)
        def _(n):
            part = lax.dot_general(
                grad_v[block], w_v[block, pl.ds(pl.multiple_of(n * TILE, TILE), TILE), :], NT,
                preferred_element_type=f32,
            )
            if first:
                hgrad[n] = part
            else:
                hgrad[n] += part

    last_z = jnp.where(z < ROWS_Z // 2, ROWS_Z - 1, 0)
    last = at(last_z, xo)

    def add_level(level):
        if level < ROWS_Z:
            for sign in (1, -1):
                far = z + sign * level

                @pl.when((far >= 0) & (far < ROWS_Z))
                def _():
                    add_block(at(far, x))
        for sign in (1, -1) if level > 1 else (1,):
            far = z + sign * (level - 1)

            @pl.when((far >= 0) & (far < ROWS_Z) & (far != last_z))
            def _():
                rest_of(at(far, xo))
                add_block(at(far, xo))

    own_block(start)

    for load in loads[1:]:
        load.wait()
    out_t = lax.dot_general(pout_v[...], grad_v[me], NT, preferred_element_type=f32)
    for p in range(nmp):
        fac_send[p, 2 * own:3 * own, :] = out_t[p * own:(p + 1) * own, :]
    acc_a[...] = jnp.dot(x_v[...], pin_v[...], preferred_element_type=f32)
    acc_b[...] = jnp.zeros_like(acc_b)

    @pl.loop(0, tiles)
    def _(n):
        cols = pl.ds(pl.multiple_of(n * TILE, TILE), TILE)

        @pl.loop(0, tokens // ROWS)
        def _(r):
            rows = pl.ds(pl.multiple_of(r * ROWS, ROWS), ROWS)
            g = gate_v[rows, cols].astype(f32)
            u = up_v[rows, cols].astype(f32)
            sig = 1.0 / (1.0 + jnp.exp(-g))
            a = g * sig
            act[n, rows, :] = a
            upslope[n, rows, :] = u * (sig * (1.0 + g * (1.0 - sig)))
            hid_tile[rows, :] = (a * u).astype(bf16)

        acc_b[...] += jnp.dot(hid_tile[...], phid_v[cols, :], preferred_element_type=f32)

    in_hid_t = jnp.concatenate([acc_a[...], acc_b[...]], axis=1).T
    for p in range(nmp):
        fac_send[p, 0:own, :] = in_hid_t[p * own:(p + 1) * own, :]
        fac_send[p, own:2 * own, :] = in_hid_t[rank + p * own:rank + (p + 1) * own, :]

    def exchange(src_of, dst, send_sems, recv_sems):
        return [
            pltpu.make_async_remote_copy(
                src_ref=src_of(peer), dst_ref=dst.at[k], send_sem=send_sems.at[k], recv_sem=recv_sems.at[k],
                device_id=(dp, peer), device_id_type=MESH,
            )
            for k, peer in enumerate(mp_peers)
        ]

    fac_copies = exchange(lambda peer: fac_send.at[peer], fac_recv, fac_ss, fac_rs)
    for copy in fac_copies:
        copy.start()

    for load in w_loads:
        load.wait()
    add_block(me, first=True)

    crossed(0, start, True)
    same_column(1, start, True)
    for copy in fac_copies:
        copy.wait_recv()
    mine = fac_send[me]
    for k in range(nmp - 1):
        mine = mine + fac_recv[k]
    full[me] = jnp.concatenate([mine[0:own], mine[2 * own:3 * own]], axis=0).astype(bf16)
    hid_own = mine[own:2 * own]
    full_copies = [
        pltpu.make_async_remote_copy(
            src_ref=full.at[me], dst_ref=full.at[me], send_sem=full_ss.at[k], recv_sem=full_rs.at[k],
            device_id=(dp, peer), device_id_type=MESH,
        )
        for k, peer in enumerate(mp_peers)
    ]
    for copy in full_copies:
        copy.start()
    add_level(1)

    crossed(1, start, True)
    same_column(2, start, True)
    add_level(2)

    crossed(2, start, True)
    same_column(3, start, True)
    add_level(3)

    for copy in full_copies:
        copy.wait_recv()
    seqs = out_ref.shape[1]
    member = (seq_v[...] == lax.broadcasted_iota(jnp.int32, (seqs, tokens), 0)).astype(f32)

    @pl.loop(0, nmp)
    def _(p):
        block = full[p].astype(f32)
        weighted[p] = jnp.concatenate([block[i:i + 1, :] * member for i in range(own)], axis=0).astype(bf16)

    out_full = jnp.concatenate([full[p].astype(f32)[own:2 * own] for p in range(nmp)], axis=0)
    weighted_hid = jnp.concatenate([hid_own[i:i + 1, :] * member for i in range(own)], axis=0)
    hid_high = weighted_hid.astype(bf16)
    hid_low = (weighted_hid - hid_high.astype(f32)).astype(bf16)
    out_bf = out_full.astype(bf16)
    raw_down = lax.dot_general(hid_high, out_bf, NT, preferred_element_type=f32) + lax.dot_general(
        hid_low, out_bf, NT, preferred_element_type=f32
    )
    crossed(3, start, True)
    rest_of(last)

    acc_a[...] = jnp.zeros_like(acc_a)
    acc_b[...] = jnp.zeros_like(acc_b)

    @pl.loop(0, tiles)
    def _(n):
        cols = pl.ds(pl.multiple_of(n * TILE, TILE), TILE)
        hgrad[n] += lax.dot_general(grad_v[last], w_v[last, cols, :], NT, preferred_element_type=f32)

        @pl.loop(0, tokens // ROWS)
        def _(r):
            rows = pl.ds(pl.multiple_of(r * ROWS, ROWS), ROWS)
            h = hgrad[n, rows, :]
            hid_tile[rows, :] = (h * upslope[n, rows, :]).astype(bf16)
            up_tile[rows, :] = (h * act[n, rows, :]).astype(bf16)

        acc_a[...] += jnp.dot(hid_tile[...], pgate_v[cols, :], preferred_element_type=f32)
        acc_b[...] += jnp.dot(up_tile[...], pup_v[cols, :], preferred_element_type=f32)

    part = jnp.concatenate([acc_a[...], acc_b[...]], axis=1)
    high = part.astype(bf16)
    low = (part - high.astype(f32)).astype(bf16)

    @pl.loop(0, nmp)
    def _(p):
        one = jnp.dot(weighted[p], high, preferred_element_type=f32) + jnp.dot(
            weighted[p], low, preferred_element_type=f32
        )
        raw_own[p] = one
        raw_send[p] = one.astype(bf16)

    raw_copies = exchange(lambda peer: raw_send.at[peer], raw_recv, raw_ss, raw_rs)
    for copy in raw_copies:
        copy.start()
    for copy in raw_copies:
        copy.wait_recv()
    raw = raw_own[me]
    for k in range(nmp - 1):
        raw = raw + raw_recv[k].astype(f32)

    sq_pair = jnp.sum(raw * raw, axis=0, keepdims=True)
    sq_down = jnp.sum(raw_down * raw_down, axis=0, keepdims=True)
    sq_mine[...] = jnp.concatenate(
        [sq_pair, jnp.concatenate([sq_down, jnp.zeros_like(sq_down)], axis=1), jnp.zeros((6, 2 * rank), f32)], axis=0
    )
    sq_copies = exchange(lambda peer: sq_mine, sq_recv, sq_ss, sq_rs)
    for copy in sq_copies:
        copy.start()
    for copy in sq_copies:
        copy.wait_recv()
    total = sq_mine[...]
    for k in range(nmp - 1):
        total = total + sq_recv[k]
    sq_group[...] = total
    dp_copies = [
        pltpu.make_async_remote_copy(
            src_ref=sq_group, dst_ref=sq_dp.at[k], send_sem=dp_ss.at[k], recv_sem=dp_rs.at[k],
            device_id=(peer, me), device_id_type=MESH,
        )
        for k, peer in enumerate(dp_peers)
    ]
    for copy in dp_copies:
        copy.start()
    for copy in dp_copies:
        copy.wait_recv()
    for k in range(ndp - 1):
        total = total + sq_dp[k]
    entries = seqs * ndp * rank * rank

    def scale(values):
        return lax.rsqrt(jnp.sum(values, axis=1, keepdims=True) / entries + 1e-06)

    scale_gate = scale(total[0:1, :rank])
    scale_up = scale(total[0:1, rank:])
    scale_down = scale(total[1:2, :])
    for q in range(own // 2):
        lanes = slice(q * 2 * rank, (q + 1) * 2 * rank)
        even = slice(2 * q * seqs, (2 * q + 1) * seqs)
        odd = slice((2 * q + 1) * seqs, (2 * q + 2) * seqs)
        out_ref[0, :, lanes] = jnp.concatenate([raw[even, :rank], raw[odd, :rank]], axis=1) * scale_gate
        out_ref[1, :, lanes] = jnp.concatenate([raw[even, rank:], raw[odd, rank:]], axis=1) * scale_up
        out_ref[2, :, lanes] = jnp.concatenate([raw_down[even], raw_down[odd]], axis=1) * scale_down

    own_block(done)
    for level in range(1, ROWS_Z):
        same_column(level, done, False)
    for dist in range(ROWS_Z):
        crossed(dist, done, False)
    for copy in fac_copies + full_copies + raw_copies + sq_copies + dp_copies:
        copy.wait_send()


def fused_device(ndp, nmp, *args):
    layer_input, gate_pre, up_pre, out_grad, w_down, proj_input, _, _, _, proj_output, seq_ids = args
    tokens, width = out_grad.shape
    units = w_down.shape[0]
    rank = proj_input.shape[1]
    own = rank // nmp
    tiles = units // TILE
    f32, bf16 = jnp.float32, jnp.bfloat16
    vmem, dma = pltpu.VMEM, pltpu.SemaphoreType.DMA
    peers, dpeers = nmp - 1, max(ndp - 1, 1)
    any_spec = pl.BlockSpec(memory_space=pl.ANY)
    result = pl.pallas_call(
        functools.partial(fused_kernel, ndp, nmp),
        out_shape=jax.ShapeDtypeStruct((3, SEQ_DEV, own * rank), f32),
        in_specs=[any_spec] * len(args),
        out_specs=pl.BlockSpec(memory_space=pltpu.VMEM),
        scratch_shapes=[
            vmem(layer_input.shape, bf16),
            vmem(gate_pre.shape, bf16),
            vmem(up_pre.shape, bf16),
            vmem((nmp, tokens, width), bf16),
            vmem((nmp, units, width), bf16),
            vmem(proj_input.shape, bf16),
            vmem((units, rank), bf16),
            vmem((units, rank), bf16),
            vmem((units, rank), bf16),
            vmem(proj_output.shape, bf16),
            vmem(seq_ids.shape, jnp.int32),
            vmem((tiles, tokens, TILE), f32),
            vmem((tiles, tokens, TILE), f32),
            vmem((tiles, tokens, TILE), f32),
            vmem((tokens, TILE), bf16),
            vmem((tokens, TILE), bf16),
            vmem((tokens, rank), f32),
            vmem((tokens, rank), f32),
            vmem((nmp, 3 * own, tokens), f32),
            vmem((peers, 3 * own, tokens), f32),
            vmem((nmp, 2 * own, tokens), bf16),
            vmem((nmp, own * SEQ_DEV, tokens), bf16),
            vmem((nmp, own * SEQ_DEV, 2 * rank), f32),
            vmem((nmp, own * SEQ_DEV, 2 * rank), bf16),
            vmem((peers, own * SEQ_DEV, 2 * rank), bf16),
            vmem((8, 2 * rank), f32),
            vmem((peers, 8, 2 * rank), f32),
            vmem((8, 2 * rank), f32),
            vmem((dpeers, 8, 2 * rank), f32),
            dma((10,)),
            dma((nmp,)),
            dma((3, nmp, PIECES)),
            dma((nmp, PIECES)),
            dma((peers,)), dma((peers,)),
            dma((peers,)), dma((peers,)),
            dma((peers,)), dma((peers,)),
            dma((peers,)), dma((peers,)),
            dma((dpeers,)), dma((dpeers,)),
        ],
        compiler_params=pltpu.CompilerParams(
            collective_id=0, has_side_effects=True, vmem_limit_bytes=56 * 1024 * 1024
        ),
        cost_estimate=pl.CostEstimate(
            flops=2 * tokens * units * width * nmp, bytes_accessed=2 * units * width * nmp,
            transcendentals=tokens * units,
        ),
    )(*args)
    return jnp.transpose(result, (1, 0, 2))


def solution(mesh):
    fits = mesh.shape["mp"] == ROWS_Z * COLS_X
    body = functools.partial(fused_device, mesh.shape["dp"], mesh.shape["mp"]) if fits else per_device
    in_specs = (
        P("dp", "mp"),
        P("dp", "mp"),
        P("dp", "mp"),
        P("dp", "mp"),
        P("mp", None),
        P("mp", None),
        P("mp", None),
        P("mp", None),
        P("mp", None),
        P(None, "mp"),
        P("dp", None),
    )
    out_specs = P("dp", None, "mp")
    return jax.shard_map(
        body, mesh=mesh, in_specs=in_specs, out_specs=out_specs, check_vma=False
    )
```

```python
import functools

import jax
import jax.numpy as jnp
from jax import lax
from jax.experimental import pallas as pl
from jax.experimental.pallas import tpu as pltpu
from jax.sharding import PartitionSpec as P

SEQ_DEV = 8


def silu_parts(gate_value):
    sigmoid_v = jax.nn.sigmoid(gate_value)
    return (gate_value * sigmoid_v, sigmoid_v * (1.0 + gate_value * (1.0 - sigmoid_v)))


def layer_features(member, left_in, left_hid, gate_factor, up_factor, out_factor):
    seq_count = member.shape[0]
    tok_rows = member.shape[1]
    left_width = left_in.shape[1]
    rank_dim = out_factor.shape[1]
    weighted_in = (member[:, None, :] * left_in.T[None, :, :]).reshape(
        seq_count * left_width, tok_rows
    )
    weighted_hid = (member[:, None, :] * left_hid.T[None, :, :]).reshape(
        seq_count * left_width, tok_rows
    )
    paired = jnp.dot(
        weighted_in,
        jnp.concatenate([gate_factor, up_factor], axis=1),
        precision=lax.Precision.HIGHEST,
    )
    paired = paired.reshape(seq_count, left_width, 2, rank_dim)
    gate_feat = paired[:, :, 0, :].reshape(seq_count, left_width * rank_dim)
    up_feat = paired[:, :, 1, :].reshape(seq_count, left_width * rank_dim)
    down_feat = jnp.dot(weighted_hid, out_factor, precision=lax.Precision.HIGHEST).reshape(
        seq_count, left_width * rank_dim
    )
    return jnp.stack([gate_feat, up_feat, down_feat], axis=1)


def per_device(
    layer_input,
    gate_pre,
    up_pre,
    out_grad,
    w_down,
    proj_input,
    proj_hidden,
    proj_gate,
    proj_upward,
    proj_output,
    seq_ids,
):
    contract = (((1,), (1,)), ((), ()))
    rank_dim = proj_input.shape[1]
    own_width = rank_dim // lax.axis_size("mp")
    position = lax.axis_index("mp")
    gate_value = gate_pre.astype(jnp.float32)
    up_value = up_pre.astype(jnp.float32)
    activated, slope_value = silu_parts(gate_value)
    hidden = (activated * up_value).astype(jnp.bfloat16)
    in_part = jnp.dot(layer_input, proj_input, preferred_element_type=jnp.float32)
    hid_part = jnp.dot(hidden, proj_hidden, preferred_element_type=jnp.float32)
    hidden_grad = lax.dot_general(
        lax.all_gather(out_grad, "mp", axis=1, tiled=True),
        w_down,
        contract,
        preferred_element_type=jnp.float32,
    )
    out_part = lax.dot_general(out_grad, proj_output, contract, preferred_element_type=jnp.float32)
    gate_grad = (hidden_grad * up_value * slope_value).astype(jnp.bfloat16)
    upward_grad = (hidden_grad * activated).astype(jnp.bfloat16)
    gate_part = jnp.dot(gate_grad, proj_gate, preferred_element_type=jnp.float32)
    up_part = jnp.dot(upward_grad, proj_upward, preferred_element_type=jnp.float32)
    gate_part, up_part = (gate_part, up_part)
    in_factor, hid_factor, gate_factor, up_factor, out_factor = lax.psum(
        (in_part, hid_part, gate_part, up_part, out_part), "mp"
    )
    member = (seq_ids[0][None, :] == jnp.arange(SEQ_DEV, dtype=jnp.int32)[:, None]).astype(
        jnp.float32
    )
    own_in = lax.dynamic_slice_in_dim(in_factor, position * own_width, own_width, 1)
    own_hid = lax.dynamic_slice_in_dim(hid_factor, position * own_width, own_width, 1)
    raw_feat = layer_features(member, own_in, own_hid, gate_factor, up_factor, out_factor)
    squares = jnp.sum(raw_feat * raw_feat, axis=(0, 2))
    total_sq = lax.psum(squares, ("dp", "mp"))
    entries = raw_feat.shape[0] * lax.axis_size("dp") * rank_dim * rank_dim
    scale_value = lax.rsqrt(total_sq / entries + 1e-06)
    return raw_feat * scale_value[None, :, None]


MESH = pl.DeviceIdType.MESH
ROWS_Z, COLS_X = 4, 2
PIECES = 8
X_FIRST = 1
TILE = 256
ROWS = 128
NT = (((1,), (1,)), ((), ()))
UP, DOWN, ACROSS = 0, 1, 2


def fused_kernel(
    ndp, nmp,
    x_hbm, gate_hbm, up_hbm, grad_hbm, w_hbm, pin_hbm, phid_hbm, pgate_hbm, pup_hbm, pout_hbm, seq_hbm,
    out_ref,
    x_v, gate_v, up_v, grad_v, w_v, pin_v, phid_v, pgate_v, pup_v, pout_v, seq_v,
    hgrad, act, upslope, hid_tile, up_tile, acc_hid, acc_a, acc_b,
    fac_send, fac_recv, full, weighted, raw_own, raw_send, raw_recv,
    sq_mine, sq_recv, sq_group, sq_dp,
    load_sem, w_sem, g_send, g_recv, fac_ss, fac_rs, full_ss, full_rs, raw_ss, raw_rs,
    sq_ss, sq_rs, dp_ss, dp_rs,
):
    dp = lax.axis_index("dp")
    me = lax.axis_index("mp")
    z, x = me // COLS_X, lax.rem(me, COLS_X)
    xo = 1 - x
    tokens, width = grad_hbm.shape
    tiles = w_hbm.shape[0] // TILE
    rank = pin_hbm.shape[0]
    own = rank // nmp
    prow = tokens // PIECES
    f32, bf16 = jnp.float32, jnp.bfloat16

    def at(zz, xx):
        return zz * COLS_X + xx

    loads = [
        pltpu.make_async_copy(src, dst, load_sem.at[i])
        for i, (src, dst) in enumerate(
            [
                (grad_hbm, grad_v.at[me]), (x_hbm, x_v), (pin_hbm, pin_v), (pout_hbm, pout_v), (seq_hbm, seq_v),
                (gate_hbm, gate_v), (up_hbm, up_v), (phid_hbm, phid_v), (pgate_hbm, pgate_v), (pup_hbm, pup_v),
            ]
        )
    ]
    for load in loads:
        load.start()
    w_loads = [
        pltpu.make_async_copy(w_hbm.at[:, pl.ds(b * width, width)], w_v.at[b], w_sem.at[b]) for b in range(nmp)
    ]
    for load in w_loads:
        load.start()

    barrier = pltpu.get_barrier_semaphore()
    mp_peers = [lax.rem(me + k, nmp) for k in range(1, nmp)]
    dp_peers = [lax.rem(dp + k, ndp) for k in range(1, ndp)]
    for peer in mp_peers:
        pl.semaphore_signal(barrier, inc=1, device_id=(dp, peer), device_id_type=MESH)
    for peer in dp_peers:
        pl.semaphore_signal(barrier, inc=1, device_id=(peer, me), device_id_type=MESH)
    loads[0].wait()
    pl.semaphore_wait(barrier, len(mp_peers) + len(dp_peers))

    def rows_of(kind, block, start, count, target):
        ref = grad_v.at[block, pl.ds(start, count), :]
        return pltpu.make_async_remote_copy(
            src_ref=ref, dst_ref=ref, send_sem=g_send.at[kind, block], recv_sem=g_recv.at[block, start // prow],
            device_id=(dp, target), device_id_type=MESH,
        )

    def piece(kind, block, c, target):
        return rows_of(kind, block, pl.multiple_of(c * prow, prow), prow, target)

    def arrived(block, c):
        piece(ACROSS, block, c, at(z, xo)).wait_recv()

    def upward(block, c):
        @pl.when(z < ROWS_Z - 1)
        def _():
            piece(UP, block, c, at(z + 1, x)).start()

    def downward(block, c):
        @pl.when(z > 0)
        def _():
            piece(DOWN, block, c, at(z - 1, x)).start()

    def across(block, c):
        piece(ACROSS, block, c, at(z, xo)).start()

    def inside(far):
        return (far >= 0) & (far < ROWS_Z)

    def pass_on(level, c):
        for sign, onward in ((1, downward), (-1, upward)):
            far = z + sign * level

            @pl.when(inside(far))
            def _():
                arrived(at(far, x), c)
                onward(at(far, x), c)

                @pl.when(c >= X_FIRST)
                def _():
                    across(at(far, x), c)

        @pl.when(c < X_FIRST)
        def _():
            if level == 1:
                block = at(z, xo)
                arrived(block, c)
                upward(block, c)
                downward(block, c)
                return
            for sign, onward in ((1, downward), (-1, upward)):
                far = z + sign * (level - 1)

                @pl.when(inside(far))
                def _():
                    arrived(at(far, xo), c)
                    onward(at(far, xo), c)

    def sent(kind, block, start, stop):
        if stop > start:
            target = {UP: at(z + 1, x), DOWN: at(z - 1, x), ACROSS: at(z, xo)}[kind]
            rows_of(kind, block, start * prow, (stop - start) * prow, target).wait_send()

    def all_sent(dist):
        for sign, kind in ((1, DOWN), (-1, UP)):
            far = z + sign * dist
            goes = z > 0 if kind == DOWN else z < ROWS_Z - 1

            @pl.when(inside(far) & goes)
            def _():
                sent(kind, at(far, x), 0, PIECES)
                sent(kind, at(far, xo), 0, X_FIRST)

            if dist > 0:
                @pl.when(inside(far))
                def _():
                    sent(ACROSS, at(far, x), X_FIRST, PIECES)
        if dist == 0:
            sent(ACROSS, me, 0, PIECES)

    def rest_of(block):
        @pl.loop(X_FIRST, PIECES)
        def _(c):
            arrived(block, c)

    def add_block(block, low, high, first=False):
        @pl.loop(low, high)
        def _(n):
            part = lax.dot_general(
                grad_v[block], w_v[block, pl.ds(pl.multiple_of(n * TILE, TILE), TILE), :], NT,
                preferred_element_type=f32,
            )
            if first:
                hgrad[n] = part
            else:
                hgrad[n] += part

    def share(c):
        return c * tiles // PIECES, (c + 1) * tiles // PIECES

    last_z = jnp.where(z < ROWS_Z // 2, ROWS_Z - 1, 0)
    last = at(last_z, xo)

    def level_blocks(level, op_near, op_far):
        if level < ROWS_Z:
            for sign in (1, -1):
                far = z + sign * level

                @pl.when(inside(far))
                def _():
                    op_near(at(far, x))
        for sign in (1, -1) if level > 1 else (1,):
            far2 = z + sign * (level - 1)

            @pl.when(inside(far2) & (far2 != last_z))
            def _():
                op_far(at(far2, xo))

    def await_level(level):
        level_blocks(level, lambda block: None, rest_of)

    def add_level(level, low, high):
        add = lambda block: add_block(block, low, high)
        level_blocks(level, add, add)

    @pl.loop(0, PIECES)
    def _(c):
        across(me, c)
        upward(me, c)
        downward(me, c)

    for load in loads[1:]:
        load.wait()
    out_t = lax.dot_general(pout_v[...], grad_v[me], NT, preferred_element_type=f32)
    for p in range(nmp):
        fac_send[p, 2 * own:3 * own, :] = out_t[p * own:(p + 1) * own, :]
    in_t = lax.dot_general(pin_v[...], x_v[...], NT, preferred_element_type=f32)
    for p in range(nmp):
        fac_send[p, 0:own, :] = in_t[p * own:(p + 1) * own, :]
    acc_hid[...] = jnp.zeros_like(acc_hid)

    @pl.loop(0, tiles)
    def _(n):
        cols = pl.ds(pl.multiple_of(n * TILE, TILE), TILE)

        @pl.loop(0, tokens // ROWS)
        def _(r):
            rows = pl.ds(pl.multiple_of(r * ROWS, ROWS), ROWS)
            g = gate_v[rows, cols].astype(f32)
            u = up_v[rows, cols].astype(f32)
            sig = 1.0 / (1.0 + jnp.exp(-g))
            a = g * sig
            act[n, rows, :] = a
            upslope[n, rows, :] = u * (sig * (1.0 + g * (1.0 - sig)))
            hid_tile[rows, :] = (a * u).astype(bf16)

        acc_hid[...] += lax.dot_general(phid_v[:, cols], hid_tile[...], NT, preferred_element_type=f32)

    for p in range(nmp):
        fac_send[p, own:2 * own, :] = acc_hid[p * own:(p + 1) * own, :]

    def exchange(src_of, dst, send_sems, recv_sems):
        return [
            pltpu.make_async_remote_copy(
                src_ref=src_of(peer), dst_ref=dst.at[k], send_sem=send_sems.at[k], recv_sem=recv_sems.at[k],
                device_id=(dp, peer), device_id_type=MESH,
            )
            for k, peer in enumerate(mp_peers)
        ]

    fac_copies = exchange(lambda peer: fac_send.at[peer], fac_recv, fac_ss, fac_rs)
    for copy in fac_copies:
        copy.start()

    for load in w_loads:
        load.wait()

    @pl.loop(0, PIECES)
    def _(c):
        pass_on(1, c)
        add_block(me, *share(c), first=True)

    await_level(1)

    @pl.loop(0, PIECES)
    def _(c):
        pass_on(2, c)
        add_level(1, *share(c))

    for copy in fac_copies:
        copy.wait_recv()
    mine = fac_send[me]
    for k in range(nmp - 1):
        mine = mine + fac_recv[k]
    full[me] = jnp.concatenate([mine[0:own], mine[2 * own:3 * own]], axis=0).astype(bf16)
    hid_own = mine[own:2 * own]
    full_copies = [
        pltpu.make_async_remote_copy(
            src_ref=full.at[me], dst_ref=full.at[me], send_sem=full_ss.at[k], recv_sem=full_rs.at[k],
            device_id=(dp, peer), device_id_type=MESH,
        )
        for k, peer in enumerate(mp_peers)
    ]
    for copy in full_copies:
        copy.start()
    await_level(2)

    @pl.loop(0, PIECES)
    def _(c):
        pass_on(3, c)
        add_level(2, *share(c))

    await_level(3)
    add_level(3, 0, tiles)

    for copy in full_copies:
        copy.wait_recv()
    seqs = out_ref.shape[1]
    member = (seq_v[...] == lax.broadcasted_iota(jnp.int32, (seqs, tokens), 0)).astype(f32)

    @pl.loop(0, nmp)
    def _(p):
        block = full[p].astype(f32)
        weighted[p] = jnp.concatenate([block[i:i + 1, :] * member for i in range(own)], axis=0).astype(bf16)

    out_full = jnp.concatenate([full[p].astype(f32)[own:2 * own] for p in range(nmp)], axis=0)
    weighted_hid = jnp.concatenate([hid_own[i:i + 1, :] * member for i in range(own)], axis=0)
    hid_high = weighted_hid.astype(bf16)
    hid_low = (weighted_hid - hid_high.astype(f32)).astype(bf16)
    out_bf = out_full.astype(bf16)
    raw_down = lax.dot_general(hid_high, out_bf, NT, preferred_element_type=f32) + lax.dot_general(
        hid_low, out_bf, NT, preferred_element_type=f32
    )
    all_sent(0)
    all_sent(1)

    acc_a[...] = jnp.zeros_like(acc_a)
    acc_b[...] = jnp.zeros_like(acc_b)

    half = tokens // 2
    for part_no in range(2):
        at_end = (z == 0) | (z == ROWS_Z - 1)
        for c in range(part_no * PIECES // 2, (part_no + 1) * PIECES // 2):
            if c < X_FIRST:
                @pl.when(at_end)
                def _():
                    arrived(last, c)
            else:
                arrived(last, c)
        span = slice(part_no * half, (part_no + 1) * half)

        @pl.loop(0, tiles)
        def _(n):
            cols = pl.ds(pl.multiple_of(n * TILE, TILE), TILE)
            hgrad[n, span, :] += lax.dot_general(
                grad_v[last, span, :], w_v[last, cols, :], NT, preferred_element_type=f32
            )

            @pl.loop(part_no * half // ROWS, (part_no + 1) * half // ROWS)
            def _(r):
                rows = pl.ds(pl.multiple_of(r * ROWS, ROWS), ROWS)
                h = hgrad[n, rows, :]
                hid_tile[rows, :] = (h * upslope[n, rows, :]).astype(bf16)
                up_tile[rows, :] = (h * act[n, rows, :]).astype(bf16)

            acc_a[span, :] += lax.dot_general(hid_tile[span, :], pgate_v[:, cols], NT, preferred_element_type=f32)
            acc_b[span, :] += lax.dot_general(up_tile[span, :], pup_v[:, cols], NT, preferred_element_type=f32)

    part = jnp.concatenate([acc_a[...], acc_b[...]], axis=1)
    high = part.astype(bf16)
    low = (part - high.astype(f32)).astype(bf16)

    @pl.loop(0, nmp)
    def _(p):
        one = jnp.dot(weighted[p], high, preferred_element_type=f32) + jnp.dot(
            weighted[p], low, preferred_element_type=f32
        )
        raw_own[p] = one
        raw_send[p] = one.astype(bf16)

    raw_copies = exchange(lambda peer: raw_send.at[peer], raw_recv, raw_ss, raw_rs)
    for copy in raw_copies:
        copy.start()
    all_sent(2)
    all_sent(3)
    for copy in fac_copies + full_copies:
        copy.wait_send()
    for copy in raw_copies:
        copy.wait_recv()
    raw = raw_own[me]
    for k in range(nmp - 1):
        raw = raw + raw_recv[k].astype(f32)

    sq_pair = jnp.sum(raw * raw, axis=0, keepdims=True)
    sq_down = jnp.sum(raw_down * raw_down, axis=0, keepdims=True)
    sq_mine[...] = jnp.concatenate(
        [sq_pair, jnp.concatenate([sq_down, jnp.zeros_like(sq_down)], axis=1), jnp.zeros((6, 2 * rank), f32)], axis=0
    )
    sq_copies = exchange(lambda peer: sq_mine, sq_recv, sq_ss, sq_rs)
    for copy in sq_copies:
        copy.start()
    for copy in sq_copies:
        copy.wait_recv()
    total = sq_mine[...]
    for k in range(nmp - 1):
        total = total + sq_recv[k]
    sq_group[...] = total
    dp_copies = [
        pltpu.make_async_remote_copy(
            src_ref=sq_group, dst_ref=sq_dp.at[k], send_sem=dp_ss.at[k], recv_sem=dp_rs.at[k],
            device_id=(peer, me), device_id_type=MESH,
        )
        for k, peer in enumerate(dp_peers)
    ]
    for copy in dp_copies:
        copy.start()
    for copy in dp_copies:
        copy.wait_recv()
    for k in range(ndp - 1):
        total = total + sq_dp[k]
    entries = seqs * ndp * rank * rank

    def scale(values):
        return lax.rsqrt(jnp.sum(values, axis=1, keepdims=True) / entries + 1e-06)

    scale_gate = scale(total[0:1, :rank])
    scale_up = scale(total[0:1, rank:])
    scale_down = scale(total[1:2, :])
    for q in range(own // 2):
        lanes = slice(q * 2 * rank, (q + 1) * 2 * rank)
        even = slice(2 * q * seqs, (2 * q + 1) * seqs)
        odd = slice((2 * q + 1) * seqs, (2 * q + 2) * seqs)
        out_ref[0, :, lanes] = jnp.concatenate([raw[even, :rank], raw[odd, :rank]], axis=1) * scale_gate
        out_ref[1, :, lanes] = jnp.concatenate([raw[even, rank:], raw[odd, rank:]], axis=1) * scale_up
        out_ref[2, :, lanes] = jnp.concatenate([raw_down[even], raw_down[odd]], axis=1) * scale_down

    for copy in raw_copies + sq_copies + dp_copies:
        copy.wait_send()


def fused_device(ndp, nmp, *args):
    layer_input, gate_pre, up_pre, out_grad, w_down, *projections, proj_output, seq_ids = args
    tokens, width = out_grad.shape
    units = w_down.shape[0]
    proj_input, proj_hidden, proj_gate, proj_upward = [proj.T for proj in projections]
    rank = proj_output.shape[0]
    own = rank // nmp
    tiles = units // TILE
    f32, bf16 = jnp.float32, jnp.bfloat16
    vmem, dma = pltpu.VMEM, pltpu.SemaphoreType.DMA
    peers, dpeers = nmp - 1, max(ndp - 1, 1)
    any_spec = pl.BlockSpec(memory_space=pl.ANY)
    result = pl.pallas_call(
        functools.partial(fused_kernel, ndp, nmp),
        out_shape=jax.ShapeDtypeStruct((3, SEQ_DEV, own * rank), f32),
        in_specs=[any_spec] * len(args),
        out_specs=pl.BlockSpec(memory_space=pltpu.VMEM),
        scratch_shapes=[
            vmem(layer_input.shape, bf16),
            vmem(gate_pre.shape, bf16),
            vmem(up_pre.shape, bf16),
            vmem((nmp, tokens, width), bf16),
            vmem((nmp, units, width), bf16),
            vmem(proj_input.shape, bf16),
            vmem((rank, units), bf16),
            vmem((rank, units), bf16),
            vmem((rank, units), bf16),
            vmem(proj_output.shape, bf16),
            vmem(seq_ids.shape, jnp.int32),
            vmem((tiles, tokens, TILE), f32),
            vmem((tiles, tokens, TILE), f32),
            vmem((tiles, tokens, TILE), f32),
            vmem((tokens, TILE), bf16),
            vmem((tokens, TILE), bf16),
            vmem((rank, tokens), f32),
            vmem((tokens, rank), f32),
            vmem((tokens, rank), f32),
            vmem((nmp, 3 * own, tokens), f32),
            vmem((peers, 3 * own, tokens), f32),
            vmem((nmp, 2 * own, tokens), bf16),
            vmem((nmp, own * SEQ_DEV, tokens), bf16),
            vmem((nmp, own * SEQ_DEV, 2 * rank), f32),
            vmem((nmp, own * SEQ_DEV, 2 * rank), bf16),
            vmem((peers, own * SEQ_DEV, 2 * rank), bf16),
            vmem((8, 2 * rank), f32),
            vmem((peers, 8, 2 * rank), f32),
            vmem((8, 2 * rank), f32),
            vmem((dpeers, 8, 2 * rank), f32),
            dma((10,)),
            dma((nmp,)),
            dma((3, nmp)),
            dma((nmp, PIECES)),
            dma((peers,)), dma((peers,)),
            dma((peers,)), dma((peers,)),
            dma((peers,)), dma((peers,)),
            dma((peers,)), dma((peers,)),
            dma((dpeers,)), dma((dpeers,)),
        ],
        compiler_params=pltpu.CompilerParams(
            collective_id=0, has_side_effects=True, vmem_limit_bytes=56 * 1024 * 1024
        ),
        cost_estimate=pl.CostEstimate(
            flops=2 * tokens * units * width * nmp, bytes_accessed=2 * units * width * nmp,
            transcendentals=tokens * units,
        ),
    )(
        layer_input, gate_pre, up_pre, out_grad, w_down, proj_input, proj_hidden, proj_gate, proj_upward, proj_output,
        seq_ids,
    )
    return jnp.transpose(result, (1, 0, 2))


def solution(mesh):
    fits = mesh.shape["mp"] == ROWS_Z * COLS_X
    body = functools.partial(fused_device, mesh.shape["dp"], mesh.shape["mp"]) if fits else per_device
    in_specs = (
        P("dp", "mp"),
        P("dp", "mp"),
        P("dp", "mp"),
        P("dp", "mp"),
        P("mp", None),
        P("mp", None),
        P("mp", None),
        P("mp", None),
        P("mp", None),
        P(None, "mp"),
        P("dp", None),
    )
    out_specs = P("dp", None, "mp")
    return jax.shard_map(
        body, mesh=mesh, in_specs=in_specs, out_specs=out_specs, check_vma=False
    )
```

```python
import functools

import jax
import jax.numpy as jnp
from jax import lax
from jax.experimental import pallas as pl
from jax.experimental.pallas import tpu as pltpu
from jax.sharding import PartitionSpec as P

SEQ_DEV = 8


def silu_parts(gate_value):
    sigmoid_v = jax.nn.sigmoid(gate_value)
    return (gate_value * sigmoid_v, sigmoid_v * (1.0 + gate_value * (1.0 - sigmoid_v)))


def layer_features(member, left_in, left_hid, gate_factor, up_factor, out_factor):
    seq_count = member.shape[0]
    tok_rows = member.shape[1]
    left_width = left_in.shape[1]
    rank_dim = out_factor.shape[1]
    weighted_in = (member[:, None, :] * left_in.T[None, :, :]).reshape(
        seq_count * left_width, tok_rows
    )
    weighted_hid = (member[:, None, :] * left_hid.T[None, :, :]).reshape(
        seq_count * left_width, tok_rows
    )
    paired = jnp.dot(
        weighted_in,
        jnp.concatenate([gate_factor, up_factor], axis=1),
        precision=lax.Precision.HIGHEST,
    )
    paired = paired.reshape(seq_count, left_width, 2, rank_dim)
    gate_feat = paired[:, :, 0, :].reshape(seq_count, left_width * rank_dim)
    up_feat = paired[:, :, 1, :].reshape(seq_count, left_width * rank_dim)
    down_feat = jnp.dot(weighted_hid, out_factor, precision=lax.Precision.HIGHEST).reshape(
        seq_count, left_width * rank_dim
    )
    return jnp.stack([gate_feat, up_feat, down_feat], axis=1)


def per_device(
    layer_input,
    gate_pre,
    up_pre,
    out_grad,
    w_down,
    proj_input,
    proj_hidden,
    proj_gate,
    proj_upward,
    proj_output,
    seq_ids,
):
    contract = (((1,), (1,)), ((), ()))
    rank_dim = proj_input.shape[1]
    own_width = rank_dim // lax.axis_size("mp")
    position = lax.axis_index("mp")
    gate_value = gate_pre.astype(jnp.float32)
    up_value = up_pre.astype(jnp.float32)
    activated, slope_value = silu_parts(gate_value)
    hidden = (activated * up_value).astype(jnp.bfloat16)
    in_part = jnp.dot(layer_input, proj_input, preferred_element_type=jnp.float32)
    hid_part = jnp.dot(hidden, proj_hidden, preferred_element_type=jnp.float32)
    hidden_grad = lax.dot_general(
        lax.all_gather(out_grad, "mp", axis=1, tiled=True),
        w_down,
        contract,
        preferred_element_type=jnp.float32,
    )
    out_part = lax.dot_general(out_grad, proj_output, contract, preferred_element_type=jnp.float32)
    gate_grad = (hidden_grad * up_value * slope_value).astype(jnp.bfloat16)
    upward_grad = (hidden_grad * activated).astype(jnp.bfloat16)
    gate_part = jnp.dot(gate_grad, proj_gate, preferred_element_type=jnp.float32)
    up_part = jnp.dot(upward_grad, proj_upward, preferred_element_type=jnp.float32)
    gate_part, up_part = (gate_part, up_part)
    in_factor, hid_factor, gate_factor, up_factor, out_factor = lax.psum(
        (in_part, hid_part, gate_part, up_part, out_part), "mp"
    )
    member = (seq_ids[0][None, :] == jnp.arange(SEQ_DEV, dtype=jnp.int32)[:, None]).astype(
        jnp.float32
    )
    own_in = lax.dynamic_slice_in_dim(in_factor, position * own_width, own_width, 1)
    own_hid = lax.dynamic_slice_in_dim(hid_factor, position * own_width, own_width, 1)
    raw_feat = layer_features(member, own_in, own_hid, gate_factor, up_factor, out_factor)
    squares = jnp.sum(raw_feat * raw_feat, axis=(0, 2))
    total_sq = lax.psum(squares, ("dp", "mp"))
    entries = raw_feat.shape[0] * lax.axis_size("dp") * rank_dim * rank_dim
    scale_value = lax.rsqrt(total_sq / entries + 1e-06)
    return raw_feat * scale_value[None, :, None]


MESH = pl.DeviceIdType.MESH
ROWS_Z, COLS_X = 4, 2
PIECES = 8
X_FIRST = 1
TILE = 256
ROWS = 128
NT = (((1,), (1,)), ((), ()))
UP, DOWN, ACROSS = 0, 1, 2


def fused_kernel(
    ndp, nmp,
    x_hbm, gate_hbm, up_hbm, grad_hbm, w_hbm, pin_hbm, phid_hbm, pgate_hbm, pup_hbm, pout_hbm, seq_hbm,
    out_ref,
    x_v, gate_v, up_v, grad_v, w_v, pin_v, phid_v, pgate_v, pup_v, pout_v, seq_v,
    grad_t, hgrad, act, upslope, hid_tile, up_tile, acc_hid, acc_a, acc_b,
    fac_send, fac_recv, full, weighted, raw_own, raw_send, raw_recv,
    sq_mine, sq_recv, sq_group, sq_dp,
    load_sem, w_sem, g_send, g_recv, fac_ss, fac_rs, full_ss, full_rs, raw_ss, raw_rs,
    sq_ss, sq_rs, dp_ss, dp_rs,
):
    dp = lax.axis_index("dp")
    me = lax.axis_index("mp")
    z, x = me // COLS_X, lax.rem(me, COLS_X)
    xo = 1 - x
    tokens, width = grad_hbm.shape
    tiles = w_hbm.shape[0] // TILE
    rank = pin_hbm.shape[0]
    own = rank // nmp
    prow = tokens // PIECES
    f32, bf16 = jnp.float32, jnp.bfloat16

    def at(zz, xx):
        return zz * COLS_X + xx

    loads = [
        pltpu.make_async_copy(src, dst, load_sem.at[i])
        for i, (src, dst) in enumerate(
            [
                (grad_hbm, grad_v.at[me]), (x_hbm, x_v), (pin_hbm, pin_v), (pout_hbm, pout_v), (seq_hbm, seq_v),
                (gate_hbm, gate_v), (up_hbm, up_v), (phid_hbm, phid_v), (pgate_hbm, pgate_v), (pup_hbm, pup_v),
            ]
        )
    ]
    for load in loads:
        load.start()
    w_loads = [
        pltpu.make_async_copy(w_hbm.at[:, pl.ds(b * width, width)], w_v.at[b], w_sem.at[b]) for b in range(nmp)
    ]
    for load in w_loads:
        load.start()

    barrier = pltpu.get_barrier_semaphore()
    mp_peers = [lax.rem(me + k, nmp) for k in range(1, nmp)]
    dp_peers = [lax.rem(dp + k, ndp) for k in range(1, ndp)]
    for peer in mp_peers:
        pl.semaphore_signal(barrier, inc=1, device_id=(dp, peer), device_id_type=MESH)
    for peer in dp_peers:
        pl.semaphore_signal(barrier, inc=1, device_id=(peer, me), device_id_type=MESH)
    loads[0].wait()
    pl.semaphore_wait(barrier, len(mp_peers) + len(dp_peers))

    def rows_of(kind, block, start, count, target):
        ref = grad_v.at[block, pl.ds(start, count), :]
        return pltpu.make_async_remote_copy(
            src_ref=ref, dst_ref=ref, send_sem=g_send.at[kind, block], recv_sem=g_recv.at[block, start // prow],
            device_id=(dp, target), device_id_type=MESH,
        )

    def piece(kind, block, c, target):
        return rows_of(kind, block, pl.multiple_of(c * prow, prow), prow, target)

    def arrived(block, c):
        piece(ACROSS, block, c, at(z, xo)).wait_recv()

    def upward(block, c):
        @pl.when(z < ROWS_Z - 1)
        def _():
            piece(UP, block, c, at(z + 1, x)).start()

    def downward(block, c):
        @pl.when(z > 0)
        def _():
            piece(DOWN, block, c, at(z - 1, x)).start()

    def across(block, c):
        piece(ACROSS, block, c, at(z, xo)).start()

    def inside(far):
        return (far >= 0) & (far < ROWS_Z)

    def pass_on(level, c):
        for sign, onward in ((1, downward), (-1, upward)):
            far = z + sign * level

            @pl.when(inside(far))
            def _():
                arrived(at(far, x), c)
                onward(at(far, x), c)

                @pl.when(c >= X_FIRST)
                def _():
                    across(at(far, x), c)

        @pl.when(c < X_FIRST)
        def _():
            if level == 1:
                block = at(z, xo)
                arrived(block, c)
                upward(block, c)
                downward(block, c)
                return
            for sign, onward in ((1, downward), (-1, upward)):
                far = z + sign * (level - 1)

                @pl.when(inside(far))
                def _():
                    arrived(at(far, xo), c)
                    onward(at(far, xo), c)

    def sent(kind, block, start, stop):
        if stop > start:
            target = {UP: at(z + 1, x), DOWN: at(z - 1, x), ACROSS: at(z, xo)}[kind]
            rows_of(kind, block, start * prow, (stop - start) * prow, target).wait_send()

    def all_sent(dist):
        for sign, kind in ((1, DOWN), (-1, UP)):
            far = z + sign * dist
            goes = z > 0 if kind == DOWN else z < ROWS_Z - 1

            @pl.when(inside(far) & goes)
            def _():
                sent(kind, at(far, x), 0, PIECES)
                sent(kind, at(far, xo), 0, X_FIRST)

            if dist > 0:
                @pl.when(inside(far))
                def _():
                    sent(ACROSS, at(far, x), X_FIRST, PIECES)
        if dist == 0:
            sent(ACROSS, me, 0, PIECES)

    def rest_of(block):
        @pl.loop(X_FIRST, PIECES)
        def _(c):
            arrived(block, c)

    def turn(block, low=0, high=tokens // ROWS):
        @pl.loop(low, high)
        def _(r):
            rows = pl.ds(pl.multiple_of(r * ROWS, ROWS), ROWS)
            grad_t[block, :, rows] = grad_v[block, rows, :].T

    def add_block(block, low, high, first=False):
        @pl.loop(low, high)
        def _(n):
            units = pl.ds(pl.multiple_of(n * TILE, TILE), TILE)
            part = jnp.dot(w_v[block, units, :], grad_t[block], preferred_element_type=f32)
            if first:
                hgrad[n] = part
            else:
                hgrad[n] += part

    def share(c):
        return c * tiles // PIECES, (c + 1) * tiles // PIECES

    last_z = jnp.where(z < ROWS_Z // 2, ROWS_Z - 1, 0)
    last = at(last_z, xo)

    def level_blocks(level, op_near, op_far):
        if level < ROWS_Z:
            for sign in (1, -1):
                far = z + sign * level

                @pl.when(inside(far))
                def _():
                    op_near(at(far, x))
        for sign in (1, -1) if level > 1 else (1,):
            far2 = z + sign * (level - 1)

            @pl.when(inside(far2) & (far2 != last_z))
            def _():
                op_far(at(far2, xo))

    def await_level(level):
        def whole(block):
            rest_of(block)
            turn(block)

        level_blocks(level, turn, whole)

    def add_level(level, low, high):
        add = lambda block: add_block(block, low, high)
        level_blocks(level, add, add)

    @pl.loop(0, PIECES)
    def _(c):
        across(me, c)
        upward(me, c)
        downward(me, c)

    for load in loads[1:]:
        load.wait()
    turn(me)
    out_t = jnp.dot(pout_v[...], grad_t[me], preferred_element_type=f32)
    for p in range(nmp):
        fac_send[p, 2 * own:3 * own, :] = out_t[p * own:(p + 1) * own, :]
    in_t = lax.dot_general(pin_v[...], x_v[...], NT, preferred_element_type=f32)
    for p in range(nmp):
        fac_send[p, 0:own, :] = in_t[p * own:(p + 1) * own, :]
    acc_hid[...] = jnp.zeros_like(acc_hid)

    @pl.loop(0, tiles)
    def _(n):
        cols = pl.ds(pl.multiple_of(n * TILE, TILE), TILE)

        @pl.loop(0, tokens // ROWS)
        def _(r):
            rows = pl.ds(pl.multiple_of(r * ROWS, ROWS), ROWS)
            g = gate_v[rows, cols].T.astype(f32)
            u = up_v[rows, cols].T.astype(f32)
            sig = 1.0 / (1.0 + jnp.exp(-g))
            a = g * sig
            act[n, :, rows] = a
            upslope[n, :, rows] = u * (sig * (1.0 + g * (1.0 - sig)))
            hid_tile[:, rows] = (a * u).astype(bf16)

        acc_hid[...] += jnp.dot(phid_v[:, cols], hid_tile[...], preferred_element_type=f32)

    for p in range(nmp):
        fac_send[p, own:2 * own, :] = acc_hid[p * own:(p + 1) * own, :]

    def exchange(src_of, dst, send_sems, recv_sems):
        return [
            pltpu.make_async_remote_copy(
                src_ref=src_of(peer), dst_ref=dst.at[k], send_sem=send_sems.at[k], recv_sem=recv_sems.at[k],
                device_id=(dp, peer), device_id_type=MESH,
            )
            for k, peer in enumerate(mp_peers)
        ]

    fac_copies = exchange(lambda peer: fac_send.at[peer], fac_recv, fac_ss, fac_rs)
    for copy in fac_copies:
        copy.start()

    for load in w_loads:
        load.wait()

    @pl.loop(0, PIECES)
    def _(c):
        pass_on(1, c)
        add_block(me, *share(c), first=True)

    await_level(1)

    @pl.loop(0, PIECES)
    def _(c):
        pass_on(2, c)
        add_level(1, *share(c))

    for copy in fac_copies:
        copy.wait_recv()
    mine = fac_send[me]
    for k in range(nmp - 1):
        mine = mine + fac_recv[k]
    full[me] = jnp.concatenate([mine[0:own], mine[2 * own:3 * own]], axis=0).astype(bf16)
    hid_own = mine[own:2 * own]
    full_copies = [
        pltpu.make_async_remote_copy(
            src_ref=full.at[me], dst_ref=full.at[me], send_sem=full_ss.at[k], recv_sem=full_rs.at[k],
            device_id=(dp, peer), device_id_type=MESH,
        )
        for k, peer in enumerate(mp_peers)
    ]
    for copy in full_copies:
        copy.start()
    await_level(2)

    @pl.loop(0, PIECES)
    def _(c):
        pass_on(3, c)
        add_level(2, *share(c))

    await_level(3)
    add_level(3, 0, tiles)

    for copy in full_copies:
        copy.wait_recv()
    seqs = out_ref.shape[1]
    member = (seq_v[...] == lax.broadcasted_iota(jnp.int32, (seqs, tokens), 0)).astype(f32)

    @pl.loop(0, nmp)
    def _(p):
        block = full[p].astype(f32)
        weighted[p] = jnp.concatenate([block[i:i + 1, :] * member for i in range(own)], axis=0).astype(bf16)

    out_full = jnp.concatenate([full[p].astype(f32)[own:2 * own] for p in range(nmp)], axis=0)
    weighted_hid = jnp.concatenate([hid_own[i:i + 1, :] * member for i in range(own)], axis=0)
    hid_high = weighted_hid.astype(bf16)
    hid_low = (weighted_hid - hid_high.astype(f32)).astype(bf16)
    out_bf = out_full.astype(bf16)
    raw_down = lax.dot_general(hid_high, out_bf, NT, preferred_element_type=f32) + lax.dot_general(
        hid_low, out_bf, NT, preferred_element_type=f32
    )
    all_sent(0)
    all_sent(1)

    acc_a[...] = jnp.zeros_like(acc_a)
    acc_b[...] = jnp.zeros_like(acc_b)

    half = tokens // 2
    for part_no in range(2):
        at_end = (z == 0) | (z == ROWS_Z - 1)
        for c in range(part_no * PIECES // 2, (part_no + 1) * PIECES // 2):
            if c < X_FIRST:
                @pl.when(at_end)
                def _():
                    arrived(last, c)
            else:
                arrived(last, c)
        span = slice(part_no * half, (part_no + 1) * half)
        turn(last, part_no * half // ROWS, (part_no + 1) * half // ROWS)

        @pl.loop(0, tiles)
        def _(n):
            cols = pl.ds(pl.multiple_of(n * TILE, TILE), TILE)
            hgrad[n, :, span] += jnp.dot(w_v[last, cols, :], grad_t[last, :, span], preferred_element_type=f32)

            @pl.loop(part_no * half // ROWS, (part_no + 1) * half // ROWS)
            def _(r):
                rows = pl.ds(pl.multiple_of(r * ROWS, ROWS), ROWS)
                h = hgrad[n, :, rows]
                hid_tile[:, rows] = (h * upslope[n, :, rows]).astype(bf16)
                up_tile[:, rows] = (h * act[n, :, rows]).astype(bf16)

            acc_a[:, span] += jnp.dot(pgate_v[:, cols], hid_tile[:, span], preferred_element_type=f32)
            acc_b[:, span] += jnp.dot(pup_v[:, cols], up_tile[:, span], preferred_element_type=f32)

    part = jnp.concatenate([acc_a[...], acc_b[...]], axis=0).T
    high = part.astype(bf16)
    low = (part - high.astype(f32)).astype(bf16)

    @pl.loop(0, nmp)
    def _(p):
        one = jnp.dot(weighted[p], high, preferred_element_type=f32) + jnp.dot(
            weighted[p], low, preferred_element_type=f32
        )
        raw_own[p] = one
        raw_send[p] = one.astype(bf16)

    raw_copies = exchange(lambda peer: raw_send.at[peer], raw_recv, raw_ss, raw_rs)
    for copy in raw_copies:
        copy.start()
    all_sent(2)
    all_sent(3)
    for copy in fac_copies + full_copies:
        copy.wait_send()
    for copy in raw_copies:
        copy.wait_recv()
    raw = raw_own[me]
    for k in range(nmp - 1):
        raw = raw + raw_recv[k].astype(f32)

    sq_pair = jnp.sum(raw * raw, axis=0, keepdims=True)
    sq_down = jnp.sum(raw_down * raw_down, axis=0, keepdims=True)
    sq_mine[...] = jnp.concatenate(
        [sq_pair, jnp.concatenate([sq_down, jnp.zeros_like(sq_down)], axis=1), jnp.zeros((6, 2 * rank), f32)], axis=0
    )
    sq_copies = exchange(lambda peer: sq_mine, sq_recv, sq_ss, sq_rs)
    for copy in sq_copies:
        copy.start()
    for copy in sq_copies:
        copy.wait_recv()
    total = sq_mine[...]
    for k in range(nmp - 1):
        total = total + sq_recv[k]
    sq_group[...] = total
    dp_copies = [
        pltpu.make_async_remote_copy(
            src_ref=sq_group, dst_ref=sq_dp.at[k], send_sem=dp_ss.at[k], recv_sem=dp_rs.at[k],
            device_id=(peer, me), device_id_type=MESH,
        )
        for k, peer in enumerate(dp_peers)
    ]
    for copy in dp_copies:
        copy.start()
    for copy in dp_copies:
        copy.wait_recv()
    for k in range(ndp - 1):
        total = total + sq_dp[k]
    entries = seqs * ndp * rank * rank

    def scale(values):
        return lax.rsqrt(jnp.sum(values, axis=1, keepdims=True) / entries + 1e-06)

    scale_gate = scale(total[0:1, :rank])
    scale_up = scale(total[0:1, rank:])
    scale_down = scale(total[1:2, :])
    for q in range(own // 2):
        lanes = slice(q * 2 * rank, (q + 1) * 2 * rank)
        even = slice(2 * q * seqs, (2 * q + 1) * seqs)
        odd = slice((2 * q + 1) * seqs, (2 * q + 2) * seqs)
        out_ref[0, :, lanes] = jnp.concatenate([raw[even, :rank], raw[odd, :rank]], axis=1) * scale_gate
        out_ref[1, :, lanes] = jnp.concatenate([raw[even, rank:], raw[odd, rank:]], axis=1) * scale_up
        out_ref[2, :, lanes] = jnp.concatenate([raw_down[even], raw_down[odd]], axis=1) * scale_down

    for copy in raw_copies + sq_copies + dp_copies:
        copy.wait_send()


def fused_device(ndp, nmp, *args):
    layer_input, gate_pre, up_pre, out_grad, w_down, *projections, proj_output, seq_ids = args
    tokens, width = out_grad.shape
    units = w_down.shape[0]
    proj_input, proj_hidden, proj_gate, proj_upward = [proj.T for proj in projections]
    rank = proj_output.shape[0]
    own = rank // nmp
    tiles = units // TILE
    f32, bf16 = jnp.float32, jnp.bfloat16
    vmem, dma = pltpu.VMEM, pltpu.SemaphoreType.DMA
    peers, dpeers = nmp - 1, max(ndp - 1, 1)
    any_spec = pl.BlockSpec(memory_space=pl.ANY)
    result = pl.pallas_call(
        functools.partial(fused_kernel, ndp, nmp),
        out_shape=jax.ShapeDtypeStruct((3, SEQ_DEV, own * rank), f32),
        in_specs=[any_spec] * len(args),
        out_specs=pl.BlockSpec(memory_space=pltpu.VMEM),
        scratch_shapes=[
            vmem(layer_input.shape, bf16),
            vmem(gate_pre.shape, bf16),
            vmem(up_pre.shape, bf16),
            vmem((nmp, tokens, width), bf16),
            vmem((nmp, units, width), bf16),
            vmem(proj_input.shape, bf16),
            vmem((rank, units), bf16),
            vmem((rank, units), bf16),
            vmem((rank, units), bf16),
            vmem(proj_output.shape, bf16),
            vmem(seq_ids.shape, jnp.int32),
            vmem((nmp, width, tokens), bf16),
            vmem((tiles, TILE, tokens), f32),
            vmem((tiles, TILE, tokens), f32),
            vmem((tiles, TILE, tokens), f32),
            vmem((TILE, tokens), bf16),
            vmem((TILE, tokens), bf16),
            vmem((rank, tokens), f32),
            vmem((rank, tokens), f32),
            vmem((rank, tokens), f32),
            vmem((nmp, 3 * own, tokens), f32),
            vmem((peers, 3 * own, tokens), f32),
            vmem((nmp, 2 * own, tokens), bf16),
            vmem((nmp, own * SEQ_DEV, tokens), bf16),
            vmem((nmp, own * SEQ_DEV, 2 * rank), f32),
            vmem((nmp, own * SEQ_DEV, 2 * rank), bf16),
            vmem((peers, own * SEQ_DEV, 2 * rank), bf16),
            vmem((8, 2 * rank), f32),
            vmem((peers, 8, 2 * rank), f32),
            vmem((8, 2 * rank), f32),
            vmem((dpeers, 8, 2 * rank), f32),
            dma((10,)),
            dma((nmp,)),
            dma((3, nmp)),
            dma((nmp, PIECES)),
            dma((peers,)), dma((peers,)),
            dma((peers,)), dma((peers,)),
            dma((peers,)), dma((peers,)),
            dma((peers,)), dma((peers,)),
            dma((dpeers,)), dma((dpeers,)),
        ],
        compiler_params=pltpu.CompilerParams(
            collective_id=0, has_side_effects=True, vmem_limit_bytes=56 * 1024 * 1024
        ),
        cost_estimate=pl.CostEstimate(
            flops=2 * tokens * units * width * nmp, bytes_accessed=2 * units * width * nmp,
            transcendentals=tokens * units,
        ),
    )(
        layer_input, gate_pre, up_pre, out_grad, w_down, proj_input, proj_hidden, proj_gate, proj_upward, proj_output,
        seq_ids,
    )
    return jnp.transpose(result, (1, 0, 2))


def solution(mesh):
    fits = mesh.shape["mp"] == ROWS_Z * COLS_X
    body = functools.partial(fused_device, mesh.shape["dp"], mesh.shape["mp"]) if fits else per_device
    in_specs = (
        P("dp", "mp"),
        P("dp", "mp"),
        P("dp", "mp"),
        P("dp", "mp"),
        P("mp", None),
        P("mp", None),
        P("mp", None),
        P("mp", None),
        P("mp", None),
        P(None, "mp"),
        P("dp", None),
    )
    out_specs = P("dp", None, "mp")
    return jax.shard_map(
        body, mesh=mesh, in_specs=in_specs, out_specs=out_specs, check_vma=False
    )
```

```python
import functools

import jax
import jax.numpy as jnp
from jax import lax
from jax.experimental import pallas as pl
from jax.experimental.pallas import tpu as pltpu
from jax.sharding import PartitionSpec as P

SEQ_DEV = 8


def silu_parts(gate_value):
    sigmoid_v = jax.nn.sigmoid(gate_value)
    return (gate_value * sigmoid_v, sigmoid_v * (1.0 + gate_value * (1.0 - sigmoid_v)))


def layer_features(member, left_in, left_hid, gate_factor, up_factor, out_factor):
    seq_count = member.shape[0]
    tok_rows = member.shape[1]
    left_width = left_in.shape[1]
    rank_dim = out_factor.shape[1]
    weighted_in = (member[:, None, :] * left_in.T[None, :, :]).reshape(
        seq_count * left_width, tok_rows
    )
    weighted_hid = (member[:, None, :] * left_hid.T[None, :, :]).reshape(
        seq_count * left_width, tok_rows
    )
    paired = jnp.dot(
        weighted_in,
        jnp.concatenate([gate_factor, up_factor], axis=1),
        precision=lax.Precision.HIGHEST,
    )
    paired = paired.reshape(seq_count, left_width, 2, rank_dim)
    gate_feat = paired[:, :, 0, :].reshape(seq_count, left_width * rank_dim)
    up_feat = paired[:, :, 1, :].reshape(seq_count, left_width * rank_dim)
    down_feat = jnp.dot(weighted_hid, out_factor, precision=lax.Precision.HIGHEST).reshape(
        seq_count, left_width * rank_dim
    )
    return jnp.stack([gate_feat, up_feat, down_feat], axis=1)


def per_device(
    layer_input,
    gate_pre,
    up_pre,
    out_grad,
    w_down,
    proj_input,
    proj_hidden,
    proj_gate,
    proj_upward,
    proj_output,
    seq_ids,
):
    contract = (((1,), (1,)), ((), ()))
    rank_dim = proj_input.shape[1]
    own_width = rank_dim // lax.axis_size("mp")
    position = lax.axis_index("mp")
    gate_value = gate_pre.astype(jnp.float32)
    up_value = up_pre.astype(jnp.float32)
    activated, slope_value = silu_parts(gate_value)
    hidden = (activated * up_value).astype(jnp.bfloat16)
    in_part = jnp.dot(layer_input, proj_input, preferred_element_type=jnp.float32)
    hid_part = jnp.dot(hidden, proj_hidden, preferred_element_type=jnp.float32)
    hidden_grad = lax.dot_general(
        lax.all_gather(out_grad, "mp", axis=1, tiled=True),
        w_down,
        contract,
        preferred_element_type=jnp.float32,
    )
    out_part = lax.dot_general(out_grad, proj_output, contract, preferred_element_type=jnp.float32)
    gate_grad = (hidden_grad * up_value * slope_value).astype(jnp.bfloat16)
    upward_grad = (hidden_grad * activated).astype(jnp.bfloat16)
    gate_part = jnp.dot(gate_grad, proj_gate, preferred_element_type=jnp.float32)
    up_part = jnp.dot(upward_grad, proj_upward, preferred_element_type=jnp.float32)
    gate_part, up_part = (gate_part, up_part)
    in_factor, hid_factor, gate_factor, up_factor, out_factor = lax.psum(
        (in_part, hid_part, gate_part, up_part, out_part), "mp"
    )
    member = (seq_ids[0][None, :] == jnp.arange(SEQ_DEV, dtype=jnp.int32)[:, None]).astype(
        jnp.float32
    )
    own_in = lax.dynamic_slice_in_dim(in_factor, position * own_width, own_width, 1)
    own_hid = lax.dynamic_slice_in_dim(hid_factor, position * own_width, own_width, 1)
    raw_feat = layer_features(member, own_in, own_hid, gate_factor, up_factor, out_factor)
    squares = jnp.sum(raw_feat * raw_feat, axis=(0, 2))
    total_sq = lax.psum(squares, ("dp", "mp"))
    entries = raw_feat.shape[0] * lax.axis_size("dp") * rank_dim * rank_dim
    scale_value = lax.rsqrt(total_sq / entries + 1e-06)
    return raw_feat * scale_value[None, :, None]


MESH = pl.DeviceIdType.MESH
ROWS_Z, COLS_X = 4, 2
PIECES = 4
TILE = 256
ROWS = 128
NT = (((1,), (1,)), ((), ()))
ACROSS = ROWS_Z


def fused_kernel(
    ndp, nmp,
    x_hbm, gate_hbm, up_hbm, grad_hbm, w_hbm, pin_hbm, phid_hbm, pgate_hbm, pup_hbm, pout_hbm, seq_hbm,
    out_ref,
    x_v, gate_v, up_v, grad_v, w_v, pin_v, phid_v, pgate_v, pup_v, pout_v, seq_v,
    grad_t, hgrad, act, upslope, hid_tile, up_tile, acc_hid, acc_a, acc_b,
    fac_send, fac_recv, full, weighted, raw_own, raw_send, raw_recv,
    sq_mine, sq_recv, sq_group, sq_dp,
    load_sem, w_sem, g_send, g_recv, fac_ss, fac_rs, full_ss, full_rs, raw_ss, raw_rs,
    sq_ss, sq_rs, dp_ss, dp_rs,
):
    dp = lax.axis_index("dp")
    me = lax.axis_index("mp")
    z, x = me // COLS_X, lax.rem(me, COLS_X)
    xo = 1 - x
    tokens, width = grad_hbm.shape
    tiles = w_hbm.shape[0] // TILE
    rank = pin_hbm.shape[0]
    own = rank // nmp
    prow = tokens // PIECES
    f32, bf16 = jnp.float32, jnp.bfloat16

    def at(zz, xx):
        return zz * COLS_X + xx

    loads = [
        pltpu.make_async_copy(src, dst, load_sem.at[i])
        for i, (src, dst) in enumerate(
            [
                (grad_hbm, grad_v.at[me]), (x_hbm, x_v), (pin_hbm, pin_v), (pout_hbm, pout_v), (seq_hbm, seq_v),
                (gate_hbm, gate_v), (up_hbm, up_v), (phid_hbm, phid_v), (pgate_hbm, pgate_v), (pup_hbm, pup_v),
            ]
        )
    ]
    for load in loads:
        load.start()
    w_loads = [
        pltpu.make_async_copy(w_hbm.at[:, pl.ds(b * width, width)], w_v.at[b], w_sem.at[b]) for b in range(nmp)
    ]
    for load in w_loads:
        load.start()

    barrier = pltpu.get_barrier_semaphore()
    mp_peers = [lax.rem(me + k, nmp) for k in range(1, nmp)]
    dp_peers = [lax.rem(dp + k, ndp) for k in range(1, ndp)]
    for peer in mp_peers:
        pl.semaphore_signal(barrier, inc=1, device_id=(dp, peer), device_id_type=MESH)
    for peer in dp_peers:
        pl.semaphore_signal(barrier, inc=1, device_id=(peer, me), device_id_type=MESH)
    loads[0].wait()
    pl.semaphore_wait(barrier, len(mp_peers) + len(dp_peers))

    def rows_of(kind, block, start, count, target):
        ref = grad_v.at[block, pl.ds(start, count), :]
        return pltpu.make_async_remote_copy(
            src_ref=ref, dst_ref=ref, send_sem=g_send.at[kind, block], recv_sem=g_recv.at[block, start // prow],
            device_id=(dp, target), device_id_type=MESH,
        )

    def piece(kind, block, c, target):
        return rows_of(kind, block, pl.multiple_of(c * prow, prow), prow, target)

    def arrived(block, c):
        piece(ACROSS, block, c, at(z, xo)).wait_recv()

    def across(block, c):
        piece(ACROSS, block, c, at(z, xo)).start()

    def along(block, c, target_z):
        piece(target_z, block, c, at(target_z, x)).start()

    def inside(far):
        return (far >= 0) & (far < ROWS_Z)

    at_end = (z == 0) | (z == ROWS_Z - 1)

    def own_targets(op):
        for dist in range(ROWS_Z - 1, 0, -1):
            for sign in (1, -1):
                target_z = z + sign * dist
                goes = inside(target_z)

                @pl.when(goes if dist == 1 else goes & at_end)
                def _():
                    op(target_z)

    def handed_on(op):
        for sign in (1, -1):
            far, target_z = z + sign, z - sign

            @pl.when(inside(far) & (far != 0) & (far != ROWS_Z - 1) & jnp.logical_not(at_end))
            def _():
                op(at(far, x), target_z)

    def pass_on(level, c):
        for sign in (1, -1):
            far = z + sign * level

            @pl.when(inside(far))
            def _():
                arrived(at(far, x), c)

        if level == 1:
            handed_on(lambda block, target_z: along(block, c, target_z))
        for sign in (1, -1):
            far = z + sign * level

            @pl.when(inside(far))
            def _():
                across(at(far, x), c)

    def sent(kind, block, target):
        rows_of(kind, block, 0, tokens, target).wait_send()

    def all_sent(dist):
        if dist == 0:
            sent(ACROSS, me, at(z, xo))
            own_targets(lambda target_z: sent(target_z, me, at(target_z, x)))
            return
        if dist == 1:
            handed_on(lambda block, target_z: sent(target_z, block, at(target_z, x)))
        for sign in (1, -1):
            far = z + sign * dist

            @pl.when(inside(far))
            def _():
                sent(ACROSS, at(far, x), at(z, xo))

    def rest_of(block):
        @pl.loop(0, PIECES)
        def _(c):
            arrived(block, c)

    def turn(block, low=0, high=tokens // ROWS):
        @pl.loop(low, high)
        def _(r):
            rows = pl.ds(pl.multiple_of(r * ROWS, ROWS), ROWS)
            grad_t[block, :, rows] = grad_v[block, rows, :].T

    def add_block(block, low, high, first=False):
        @pl.loop(low, high)
        def _(n):
            units = pl.ds(pl.multiple_of(n * TILE, TILE), TILE)
            part = jnp.dot(w_v[block, units, :], grad_t[block], preferred_element_type=f32)
            if first:
                hgrad[n] = part
            else:
                hgrad[n] += part

    def share(c):
        return c * tiles // PIECES, (c + 1) * tiles // PIECES

    last_z = jnp.where(z < ROWS_Z // 2, ROWS_Z - 1, 0)
    last = at(last_z, xo)

    def level_blocks(level, op_near, op_far):
        if level < ROWS_Z:
            for sign in (1, -1):
                far = z + sign * level

                @pl.when(inside(far))
                def _():
                    op_near(at(far, x))
        for sign in (1, -1) if level > 1 else (1,):
            far2 = z + sign * (level - 1)

            @pl.when(inside(far2) & (far2 != last_z))
            def _():
                op_far(at(far2, xo))

    def await_level(level):
        def whole(block):
            rest_of(block)
            turn(block)

        level_blocks(level, turn, whole)

    def add_level(level, low, high):
        add = lambda block: add_block(block, low, high)
        level_blocks(level, add, add)

    @pl.loop(0, PIECES)
    def _(c):
        own_targets(lambda target_z: along(me, c, target_z))
        across(me, c)

    for load in loads[1:]:
        load.wait()
    turn(me)
    out_t = jnp.dot(pout_v[...], grad_t[me], preferred_element_type=f32)
    for p in range(nmp):
        fac_send[p, 2 * own:3 * own, :] = out_t[p * own:(p + 1) * own, :]
    in_t = lax.dot_general(pin_v[...], x_v[...], NT, preferred_element_type=f32)
    for p in range(nmp):
        fac_send[p, 0:own, :] = in_t[p * own:(p + 1) * own, :]
    acc_hid[...] = jnp.zeros_like(acc_hid)

    @pl.loop(0, tiles)
    def _(n):
        cols = pl.ds(pl.multiple_of(n * TILE, TILE), TILE)

        @pl.loop(0, tokens // ROWS)
        def _(r):
            rows = pl.ds(pl.multiple_of(r * ROWS, ROWS), ROWS)
            g = gate_v[rows, cols].T.astype(f32)
            u = up_v[rows, cols].T.astype(f32)
            sig = 1.0 / (1.0 + jnp.exp(-g))
            a = g * sig
            act[n, :, rows] = a
            upslope[n, :, rows] = u * (sig * (1.0 + g * (1.0 - sig)))
            hid_tile[:, rows] = (a * u).astype(bf16)

        acc_hid[...] += jnp.dot(phid_v[:, cols], hid_tile[...], preferred_element_type=f32)

    for p in range(nmp):
        fac_send[p, own:2 * own, :] = acc_hid[p * own:(p + 1) * own, :]

    def exchange(src_of, dst, send_sems, recv_sems):
        return [
            pltpu.make_async_remote_copy(
                src_ref=src_of(peer), dst_ref=dst.at[k], send_sem=send_sems.at[k], recv_sem=recv_sems.at[k],
                device_id=(dp, peer), device_id_type=MESH,
            )
            for k, peer in enumerate(mp_peers)
        ]

    fac_copies = exchange(lambda peer: fac_send.at[peer], fac_recv, fac_ss, fac_rs)
    for copy in fac_copies:
        copy.start()

    for load in w_loads:
        load.wait()

    @pl.loop(0, PIECES)
    def _(c):
        pass_on(1, c)
        add_block(me, *share(c), first=True)

    await_level(1)

    @pl.loop(0, PIECES)
    def _(c):
        pass_on(2, c)
        add_level(1, *share(c))

    for copy in fac_copies:
        copy.wait_recv()
    mine = fac_send[me]
    for k in range(nmp - 1):
        mine = mine + fac_recv[k]
    full[me] = jnp.concatenate([mine[0:own], mine[2 * own:3 * own]], axis=0).astype(bf16)
    hid_own = mine[own:2 * own]
    full_copies = [
        pltpu.make_async_remote_copy(
            src_ref=full.at[me], dst_ref=full.at[me], send_sem=full_ss.at[k], recv_sem=full_rs.at[k],
            device_id=(dp, peer), device_id_type=MESH,
        )
        for k, peer in enumerate(mp_peers)
    ]
    for copy in full_copies:
        copy.start()
    await_level(2)

    @pl.loop(0, PIECES)
    def _(c):
        pass_on(3, c)
        add_level(2, *share(c))

    await_level(3)
    add_level(3, 0, tiles)

    for copy in full_copies:
        copy.wait_recv()
    seqs = out_ref.shape[1]
    member = (seq_v[...] == lax.broadcasted_iota(jnp.int32, (seqs, tokens), 0)).astype(f32)

    @pl.loop(0, nmp)
    def _(p):
        block = full[p].astype(f32)
        weighted[p] = jnp.concatenate([block[i:i + 1, :] * member for i in range(own)], axis=0).astype(bf16)

    out_full = jnp.concatenate([full[p].astype(f32)[own:2 * own] for p in range(nmp)], axis=0)
    weighted_hid = jnp.concatenate([hid_own[i:i + 1, :] * member for i in range(own)], axis=0)
    hid_high = weighted_hid.astype(bf16)
    hid_low = (weighted_hid - hid_high.astype(f32)).astype(bf16)
    out_bf = out_full.astype(bf16)
    raw_down = lax.dot_general(hid_high, out_bf, NT, preferred_element_type=f32) + lax.dot_general(
        hid_low, out_bf, NT, preferred_element_type=f32
    )
    all_sent(0)
    all_sent(1)

    acc_a[...] = jnp.zeros_like(acc_a)
    acc_b[...] = jnp.zeros_like(acc_b)

    half = tokens // 2
    for part_no in range(2):
        for c in range(part_no * PIECES // 2, (part_no + 1) * PIECES // 2):
            arrived(last, c)
        span = slice(part_no * half, (part_no + 1) * half)
        turn(last, part_no * half // ROWS, (part_no + 1) * half // ROWS)

        @pl.loop(0, tiles)
        def _(n):
            cols = pl.ds(pl.multiple_of(n * TILE, TILE), TILE)
            hgrad[n, :, span] += jnp.dot(w_v[last, cols, :], grad_t[last, :, span], preferred_element_type=f32)

            @pl.loop(part_no * half // ROWS, (part_no + 1) * half // ROWS)
            def _(r):
                rows = pl.ds(pl.multiple_of(r * ROWS, ROWS), ROWS)
                h = hgrad[n, :, rows]
                hid_tile[:, rows] = (h * upslope[n, :, rows]).astype(bf16)
                up_tile[:, rows] = (h * act[n, :, rows]).astype(bf16)

            acc_a[:, span] += jnp.dot(pgate_v[:, cols], hid_tile[:, span], preferred_element_type=f32)
            acc_b[:, span] += jnp.dot(pup_v[:, cols], up_tile[:, span], preferred_element_type=f32)

    part = jnp.concatenate([acc_a[...], acc_b[...]], axis=0).T
    high = part.astype(bf16)
    low = (part - high.astype(f32)).astype(bf16)

    @pl.loop(0, nmp)
    def _(p):
        one = jnp.dot(weighted[p], high, preferred_element_type=f32) + jnp.dot(
            weighted[p], low, preferred_element_type=f32
        )
        raw_own[p] = one
        raw_send[p] = one.astype(bf16)

    raw_copies = exchange(lambda peer: raw_send.at[peer], raw_recv, raw_ss, raw_rs)
    for copy in raw_copies:
        copy.start()
    all_sent(2)
    all_sent(3)
    for copy in fac_copies + full_copies:
        copy.wait_send()
    for copy in raw_copies:
        copy.wait_recv()
    raw = raw_own[me]
    for k in range(nmp - 1):
        raw = raw + raw_recv[k].astype(f32)

    sq_pair = jnp.sum(raw * raw, axis=0, keepdims=True)
    sq_down = jnp.sum(raw_down * raw_down, axis=0, keepdims=True)
    sq_mine[...] = jnp.concatenate(
        [sq_pair, jnp.concatenate([sq_down, jnp.zeros_like(sq_down)], axis=1), jnp.zeros((6, 2 * rank), f32)], axis=0
    )
    sq_copies = exchange(lambda peer: sq_mine, sq_recv, sq_ss, sq_rs)
    for copy in sq_copies:
        copy.start()
    for copy in sq_copies:
        copy.wait_recv()
    total = sq_mine[...]
    for k in range(nmp - 1):
        total = total + sq_recv[k]
    sq_group[...] = total
    dp_copies = [
        pltpu.make_async_remote_copy(
            src_ref=sq_group, dst_ref=sq_dp.at[k], send_sem=dp_ss.at[k], recv_sem=dp_rs.at[k],
            device_id=(peer, me), device_id_type=MESH,
        )
        for k, peer in enumerate(dp_peers)
    ]
    for copy in dp_copies:
        copy.start()
    for copy in dp_copies:
        copy.wait_recv()
    for k in range(ndp - 1):
        total = total + sq_dp[k]
    entries = seqs * ndp * rank * rank

    def scale(values):
        return lax.rsqrt(jnp.sum(values, axis=1, keepdims=True) / entries + 1e-06)

    scale_gate = scale(total[0:1, :rank])
    scale_up = scale(total[0:1, rank:])
    scale_down = scale(total[1:2, :])
    for q in range(own // 2):
        lanes = slice(q * 2 * rank, (q + 1) * 2 * rank)
        even = slice(2 * q * seqs, (2 * q + 1) * seqs)
        odd = slice((2 * q + 1) * seqs, (2 * q + 2) * seqs)
        out_ref[0, :, lanes] = jnp.concatenate([raw[even, :rank], raw[odd, :rank]], axis=1) * scale_gate
        out_ref[1, :, lanes] = jnp.concatenate([raw[even, rank:], raw[odd, rank:]], axis=1) * scale_up
        out_ref[2, :, lanes] = jnp.concatenate([raw_down[even], raw_down[odd]], axis=1) * scale_down

    for copy in raw_copies + sq_copies + dp_copies:
        copy.wait_send()


def fused_device(ndp, nmp, *args):
    layer_input, gate_pre, up_pre, out_grad, w_down, *projections, proj_output, seq_ids = args
    tokens, width = out_grad.shape
    units = w_down.shape[0]
    proj_input, proj_hidden, proj_gate, proj_upward = [proj.T for proj in projections]
    rank = proj_output.shape[0]
    own = rank // nmp
    tiles = units // TILE
    f32, bf16 = jnp.float32, jnp.bfloat16
    vmem, dma = pltpu.VMEM, pltpu.SemaphoreType.DMA
    peers, dpeers = nmp - 1, max(ndp - 1, 1)
    any_spec = pl.BlockSpec(memory_space=pl.ANY)
    result = pl.pallas_call(
        functools.partial(fused_kernel, ndp, nmp),
        out_shape=jax.ShapeDtypeStruct((3, SEQ_DEV, own * rank), f32),
        in_specs=[any_spec] * len(args),
        out_specs=pl.BlockSpec(memory_space=pltpu.VMEM),
        scratch_shapes=[
            vmem(layer_input.shape, bf16),
            vmem(gate_pre.shape, bf16),
            vmem(up_pre.shape, bf16),
            vmem((nmp, tokens, width), bf16),
            vmem((nmp, units, width), bf16),
            vmem(proj_input.shape, bf16),
            vmem((rank, units), bf16),
            vmem((rank, units), bf16),
            vmem((rank, units), bf16),
            vmem(proj_output.shape, bf16),
            vmem(seq_ids.shape, jnp.int32),
            vmem((nmp, width, tokens), bf16),
            vmem((tiles, TILE, tokens), f32),
            vmem((tiles, TILE, tokens), f32),
            vmem((tiles, TILE, tokens), f32),
            vmem((TILE, tokens), bf16),
            vmem((TILE, tokens), bf16),
            vmem((rank, tokens), f32),
            vmem((rank, tokens), f32),
            vmem((rank, tokens), f32),
            vmem((nmp, 3 * own, tokens), f32),
            vmem((peers, 3 * own, tokens), f32),
            vmem((nmp, 2 * own, tokens), bf16),
            vmem((nmp, own * SEQ_DEV, tokens), bf16),
            vmem((nmp, own * SEQ_DEV, 2 * rank), f32),
            vmem((nmp, own * SEQ_DEV, 2 * rank), bf16),
            vmem((peers, own * SEQ_DEV, 2 * rank), bf16),
            vmem((8, 2 * rank), f32),
            vmem((peers, 8, 2 * rank), f32),
            vmem((8, 2 * rank), f32),
            vmem((dpeers, 8, 2 * rank), f32),
            dma((10,)),
            dma((nmp,)),
            dma((ROWS_Z + 1, nmp)),
            dma((nmp, PIECES)),
            dma((peers,)), dma((peers,)),
            dma((peers,)), dma((peers,)),
            dma((peers,)), dma((peers,)),
            dma((peers,)), dma((peers,)),
            dma((dpeers,)), dma((dpeers,)),
        ],
        compiler_params=pltpu.CompilerParams(
            collective_id=0, has_side_effects=True, vmem_limit_bytes=56 * 1024 * 1024
        ),
        cost_estimate=pl.CostEstimate(
            flops=2 * tokens * units * width * nmp, bytes_accessed=2 * units * width * nmp,
            transcendentals=tokens * units,
        ),
    )(
        layer_input, gate_pre, up_pre, out_grad, w_down, proj_input, proj_hidden, proj_gate, proj_upward, proj_output,
        seq_ids,
    )
    return jnp.transpose(result, (1, 0, 2))


def solution(mesh):
    fits = mesh.shape["mp"] == ROWS_Z * COLS_X
    body = functools.partial(fused_device, mesh.shape["dp"], mesh.shape["mp"]) if fits else per_device
    in_specs = (
        P("dp", "mp"),
        P("dp", "mp"),
        P("dp", "mp"),
        P("dp", "mp"),
        P("mp", None),
        P("mp", None),
        P("mp", None),
        P("mp", None),
        P("mp", None),
        P(None, "mp"),
        P("dp", None),
    )
    out_specs = P("dp", None, "mp")
    return jax.shard_map(
        body, mesh=mesh, in_specs=in_specs, out_specs=out_specs, check_vma=False
    )
```

```python
import functools

import jax
import jax.numpy as jnp
from jax import lax
from jax.experimental import pallas as pl
from jax.experimental.pallas import tpu as pltpu
from jax.sharding import PartitionSpec as P

SEQ_DEV = 8


def silu_parts(gate_value):
    sigmoid_v = jax.nn.sigmoid(gate_value)
    return (gate_value * sigmoid_v, sigmoid_v * (1.0 + gate_value * (1.0 - sigmoid_v)))


def layer_features(member, left_in, left_hid, gate_factor, up_factor, out_factor):
    seq_count = member.shape[0]
    tok_rows = member.shape[1]
    left_width = left_in.shape[1]
    rank_dim = out_factor.shape[1]
    weighted_in = (member[:, None, :] * left_in.T[None, :, :]).reshape(
        seq_count * left_width, tok_rows
    )
    weighted_hid = (member[:, None, :] * left_hid.T[None, :, :]).reshape(
        seq_count * left_width, tok_rows
    )
    paired = jnp.dot(
        weighted_in,
        jnp.concatenate([gate_factor, up_factor], axis=1),
        precision=lax.Precision.HIGHEST,
    )
    paired = paired.reshape(seq_count, left_width, 2, rank_dim)
    gate_feat = paired[:, :, 0, :].reshape(seq_count, left_width * rank_dim)
    up_feat = paired[:, :, 1, :].reshape(seq_count, left_width * rank_dim)
    down_feat = jnp.dot(weighted_hid, out_factor, precision=lax.Precision.HIGHEST).reshape(
        seq_count, left_width * rank_dim
    )
    return jnp.stack([gate_feat, up_feat, down_feat], axis=1)


def per_device(
    layer_input,
    gate_pre,
    up_pre,
    out_grad,
    w_down,
    proj_input,
    proj_hidden,
    proj_gate,
    proj_upward,
    proj_output,
    seq_ids,
):
    contract = (((1,), (1,)), ((), ()))
    rank_dim = proj_input.shape[1]
    own_width = rank_dim // lax.axis_size("mp")
    position = lax.axis_index("mp")
    gate_value = gate_pre.astype(jnp.float32)
    up_value = up_pre.astype(jnp.float32)
    activated, slope_value = silu_parts(gate_value)
    hidden = (activated * up_value).astype(jnp.bfloat16)
    in_part = jnp.dot(layer_input, proj_input, preferred_element_type=jnp.float32)
    hid_part = jnp.dot(hidden, proj_hidden, preferred_element_type=jnp.float32)
    hidden_grad = lax.dot_general(
        lax.all_gather(out_grad, "mp", axis=1, tiled=True),
        w_down,
        contract,
        preferred_element_type=jnp.float32,
    )
    out_part = lax.dot_general(out_grad, proj_output, contract, preferred_element_type=jnp.float32)
    gate_grad = (hidden_grad * up_value * slope_value).astype(jnp.bfloat16)
    upward_grad = (hidden_grad * activated).astype(jnp.bfloat16)
    gate_part = jnp.dot(gate_grad, proj_gate, preferred_element_type=jnp.float32)
    up_part = jnp.dot(upward_grad, proj_upward, preferred_element_type=jnp.float32)
    gate_part, up_part = (gate_part, up_part)
    in_factor, hid_factor, gate_factor, up_factor, out_factor = lax.psum(
        (in_part, hid_part, gate_part, up_part, out_part), "mp"
    )
    member = (seq_ids[0][None, :] == jnp.arange(SEQ_DEV, dtype=jnp.int32)[:, None]).astype(
        jnp.float32
    )
    own_in = lax.dynamic_slice_in_dim(in_factor, position * own_width, own_width, 1)
    own_hid = lax.dynamic_slice_in_dim(hid_factor, position * own_width, own_width, 1)
    raw_feat = layer_features(member, own_in, own_hid, gate_factor, up_factor, out_factor)
    squares = jnp.sum(raw_feat * raw_feat, axis=(0, 2))
    total_sq = lax.psum(squares, ("dp", "mp"))
    entries = raw_feat.shape[0] * lax.axis_size("dp") * rank_dim * rank_dim
    scale_value = lax.rsqrt(total_sq / entries + 1e-06)
    return raw_feat * scale_value[None, :, None]


MESH = pl.DeviceIdType.MESH
ROWS_Z, COLS_X = 4, 2
PIECES = 8
X_FIRST = 1
TILE = 256
ROWS = 128
NT = (((1,), (1,)), ((), ()))
UP, DOWN, ACROSS = 0, 1, 2


def fused_kernel(
    ndp, nmp,
    x_hbm, gate_hbm, up_hbm, grad_hbm, w_hbm, pin_hbm, phid_hbm, pgate_hbm, pup_hbm, pout_hbm, seq_hbm,
    out_ref,
    x_v, gate_v, up_v, grad_v, w_v, pin_v, phid_v, pgate_v, pup_v, pout_v, seq_v,
    grad_t, hgrad, act, upslope, hid_tile, up_tile, acc_hid, acc_a, acc_b,
    fac_send, fac_recv, pair_send, pair_recv, hid_own, raw_down_v, full, weighted, raw_own, raw_send, raw_recv,
    sq_mine, sq_recv, sq_group, sq_dp,
    load_sem, w_sem, g_send, g_recv, fac_ss, fac_rs, pair_ss, pair_rs, full_ss, full_rs, raw_ss, raw_rs,
    sq_ss, sq_rs, dp_ss, dp_rs,
):
    dp = lax.axis_index("dp")
    me = lax.axis_index("mp")
    z, x = me // COLS_X, lax.rem(me, COLS_X)
    xo = 1 - x
    tokens, width = grad_hbm.shape
    tiles = w_hbm.shape[0] // TILE
    rank = pin_hbm.shape[0]
    own = rank // nmp
    prow = tokens // PIECES
    f32, bf16 = jnp.float32, jnp.bfloat16

    def at(zz, xx):
        return zz * COLS_X + xx

    loads = [
        pltpu.make_async_copy(src, dst, load_sem.at[i])
        for i, (src, dst) in enumerate(
            [
                (grad_hbm, grad_v.at[me]), (x_hbm, x_v), (pin_hbm, pin_v), (pout_hbm, pout_v), (seq_hbm, seq_v),
                (gate_hbm, gate_v), (up_hbm, up_v), (phid_hbm, phid_v), (pgate_hbm, pgate_v), (pup_hbm, pup_v),
            ]
        )
    ]
    for load in loads:
        load.start()
    w_loads = [
        pltpu.make_async_copy(w_hbm.at[:, pl.ds(b * width, width)], w_v.at[b], w_sem.at[b]) for b in range(nmp)
    ]
    for load in w_loads:
        load.start()

    barrier = pltpu.get_barrier_semaphore()
    mp_peers = [lax.rem(me + k, nmp) for k in range(1, nmp)]
    dp_peers = [lax.rem(dp + k, ndp) for k in range(1, ndp)]
    for peer in mp_peers:
        pl.semaphore_signal(barrier, inc=1, device_id=(dp, peer), device_id_type=MESH)
    for peer in dp_peers:
        pl.semaphore_signal(barrier, inc=1, device_id=(peer, me), device_id_type=MESH)
    loads[0].wait()
    pl.semaphore_wait(barrier, len(mp_peers) + len(dp_peers))

    def rows_of(kind, block, start, count, target):
        ref = grad_v.at[block, pl.ds(start, count), :]
        return pltpu.make_async_remote_copy(
            src_ref=ref, dst_ref=ref, send_sem=g_send.at[kind, block], recv_sem=g_recv.at[block, start // prow],
            device_id=(dp, target), device_id_type=MESH,
        )

    def piece(kind, block, c, target):
        return rows_of(kind, block, pl.multiple_of(c * prow, prow), prow, target)

    def arrived(block, c):
        piece(ACROSS, block, c, at(z, xo)).wait_recv()

    def upward(block, c):
        @pl.when(z < ROWS_Z - 1)
        def _():
            piece(UP, block, c, at(z + 1, x)).start()

    def downward(block, c):
        @pl.when(z > 0)
        def _():
            piece(DOWN, block, c, at(z - 1, x)).start()

    def across(block, c):
        piece(ACROSS, block, c, at(z, xo)).start()

    def inside(far):
        return (far >= 0) & (far < ROWS_Z)

    per_turn = max(ROWS // prow, 1)

    def turn(block, low=0, high=tokens // ROWS):
        @pl.loop(low, high)
        def _(r):
            rows = pl.ds(pl.multiple_of(r * ROWS, ROWS), ROWS)
            grad_t[block, :, rows] = grad_v[block, rows, :].T

    def pass_on(level, c):
        for sign, onward in ((1, downward), (-1, upward)):
            far = z + sign * level

            @pl.when(inside(far))
            def _():
                arrived(at(far, x), c)
                onward(at(far, x), c)

                @pl.when(c >= X_FIRST)
                def _():
                    across(at(far, x), c)

                @pl.when(lax.rem(c, per_turn) == per_turn - 1)
                def _():
                    turn(at(far, x), c // per_turn, c // per_turn + 1)

        @pl.when(c < X_FIRST)
        def _():
            if level == 1:
                block = at(z, xo)
                arrived(block, c)
                upward(block, c)
                downward(block, c)
                return
            for sign, onward in ((1, downward), (-1, upward)):
                far = z + sign * (level - 1)

                @pl.when(inside(far))
                def _():
                    arrived(at(far, xo), c)
                    onward(at(far, xo), c)

    def sent(kind, block, start, stop):
        if stop > start:
            target = {UP: at(z + 1, x), DOWN: at(z - 1, x), ACROSS: at(z, xo)}[kind]
            rows_of(kind, block, start * prow, (stop - start) * prow, target).wait_send()

    def all_sent(dist):
        for sign, kind in ((1, DOWN), (-1, UP)):
            far = z + sign * dist
            goes = z > 0 if kind == DOWN else z < ROWS_Z - 1

            @pl.when(inside(far) & goes)
            def _():
                sent(kind, at(far, x), 0, PIECES)
                sent(kind, at(far, xo), 0, X_FIRST)

            if dist > 0:
                @pl.when(inside(far))
                def _():
                    sent(ACROSS, at(far, x), X_FIRST, PIECES)
        if dist == 0:
            sent(ACROSS, me, 0, PIECES)

    def rest_of(block):
        @pl.loop(X_FIRST, PIECES)
        def _(c):
            arrived(block, c)

    def add_block(block, low, high, first=False):
        @pl.loop(low, high)
        def _(n):
            units = pl.ds(pl.multiple_of(n * TILE, TILE), TILE)
            part = jnp.dot(w_v[block, units, :], grad_t[block], preferred_element_type=f32)
            if first:
                hgrad[n] = part
            else:
                hgrad[n] += part

    def share(c):
        return c * tiles // PIECES, (c + 1) * tiles // PIECES

    last_z = jnp.where(z < ROWS_Z // 2, ROWS_Z - 1, 0)
    last = at(last_z, xo)

    def level_blocks(level, op_near, op_far):
        if level < ROWS_Z:
            for sign in (1, -1):
                far = z + sign * level

                @pl.when(inside(far))
                def _():
                    op_near(at(far, x))
        for sign in (1, -1) if level > 1 else (1,):
            far2 = z + sign * (level - 1)

            @pl.when(inside(far2) & (far2 != last_z))
            def _():
                op_far(at(far2, xo))

    def await_level(level):
        def whole(block):
            rest_of(block)
            turn(block)

        level_blocks(level, lambda block: None, whole)

    def add_level(level, low, high):
        add = lambda block: add_block(block, low, high)
        level_blocks(level, add, add)

    @pl.loop(0, PIECES)
    def _(c):
        across(me, c)
        upward(me, c)
        downward(me, c)

    for load in loads[1:]:
        load.wait()
    turn(me)
    out_t = jnp.dot(pout_v[...], grad_t[me], preferred_element_type=f32)
    for p in range(nmp):
        pair_send[p, own:2 * own, :] = out_t[p * own:(p + 1) * own, :].astype(bf16)
    in_t = lax.dot_general(pin_v[...], x_v[...], NT, preferred_element_type=f32)
    for p in range(nmp):
        fac_send[p, 0:own, :] = in_t[p * own:(p + 1) * own, :]
    acc_hid[...] = jnp.zeros_like(acc_hid)

    @pl.loop(0, tiles)
    def _(n):
        cols = pl.ds(pl.multiple_of(n * TILE, TILE), TILE)

        @pl.loop(0, tokens // ROWS)
        def _(r):
            rows = pl.ds(pl.multiple_of(r * ROWS, ROWS), ROWS)
            g = gate_v[rows, cols].T.astype(f32)
            u = up_v[rows, cols].T.astype(f32)
            sig = 1.0 / (1.0 + jnp.exp(-g))
            a = g * sig
            act[n, :, rows] = a
            upslope[n, :, rows] = u * (sig * (1.0 + g * (1.0 - sig)))
            hid_tile[:, rows] = (a * u).astype(bf16)

        acc_hid[...] += jnp.dot(phid_v[:, cols], hid_tile[...], preferred_element_type=f32)

    for p in range(nmp):
        pair_send[p, 0:own, :] = acc_hid[p * own:(p + 1) * own, :].astype(bf16)

    def exchange(src_of, dst, send_sems, recv_sems):
        return [
            pltpu.make_async_remote_copy(
                src_ref=src_of(peer), dst_ref=dst.at[k], send_sem=send_sems.at[k], recv_sem=recv_sems.at[k],
                device_id=(dp, peer), device_id_type=MESH,
            )
            for k, peer in enumerate(mp_peers)
        ]

    fac_copies = exchange(lambda peer: fac_send.at[peer], fac_recv, fac_ss, fac_rs)
    fac_copies += exchange(lambda peer: pair_send.at[peer], pair_recv, pair_ss, pair_rs)
    for copy in fac_copies:
        copy.start()

    for load in w_loads:
        load.wait()

    @pl.loop(0, PIECES)
    def _(c):
        pass_on(1, c)
        add_block(me, *share(c), first=True)

    await_level(1)

    @pl.loop(0, PIECES)
    def _(c):
        pass_on(2, c)
        add_level(1, *share(c))

    for copy in fac_copies:
        copy.wait_recv()
    mine = fac_send[me]
    pair = pair_send[me].astype(f32)
    for k in range(nmp - 1):
        mine = mine + fac_recv[k]
        pair = pair + pair_recv[k].astype(f32)
    full[me] = jnp.concatenate([mine, pair[own:]], axis=0).astype(bf16)
    hid_own[...] = pair[:own]
    full_copies = [
        pltpu.make_async_remote_copy(
            src_ref=full.at[me], dst_ref=full.at[me], send_sem=full_ss.at[k], recv_sem=full_rs.at[k],
            device_id=(dp, peer), device_id_type=MESH,
        )
        for k, peer in enumerate(mp_peers)
    ]
    for copy in full_copies:
        copy.start()
    await_level(2)

    @pl.loop(0, PIECES // 2)
    def _(c):
        pass_on(3, c)
        add_level(2, *share(c))

    for copy in full_copies:
        copy.wait_recv()
    seqs = out_ref.shape[1]
    member = (seq_v[...] == lax.broadcasted_iota(jnp.int32, (seqs, tokens), 0)).astype(f32)

    @pl.loop(0, nmp)
    def _(p):
        block = full[p].astype(f32)
        weighted[p] = jnp.concatenate([block[i:i + 1, :] * member for i in range(own)], axis=0).astype(bf16)

    out_full = jnp.concatenate([full[p].astype(f32)[own:2 * own] for p in range(nmp)], axis=0)
    weighted_hid = jnp.concatenate([hid_own[i:i + 1, :] * member for i in range(own)], axis=0)
    hid_high = weighted_hid.astype(bf16)
    hid_low = (weighted_hid - hid_high.astype(f32)).astype(bf16)
    out_bf = out_full.astype(bf16)
    raw_down_v[...] = lax.dot_general(hid_high, out_bf, NT, preferred_element_type=f32) + lax.dot_general(
        hid_low, out_bf, NT, preferred_element_type=f32
    )

    @pl.loop(PIECES // 2, PIECES)
    def _(c):
        pass_on(3, c)
        add_level(2, *share(c))

    await_level(3)
    add_level(3, 0, tiles)

    all_sent(0)
    all_sent(1)

    acc_a[...] = jnp.zeros_like(acc_a)
    acc_b[...] = jnp.zeros_like(acc_b)

    half = tokens // 2
    for part_no in range(2):
        at_end = (z == 0) | (z == ROWS_Z - 1)
        for c in range(part_no * PIECES // 2, (part_no + 1) * PIECES // 2):
            if c < X_FIRST:
                @pl.when(at_end)
                def _():
                    arrived(last, c)
            else:
                arrived(last, c)
        span = slice(part_no * half, (part_no + 1) * half)
        turn(last, part_no * half // ROWS, (part_no + 1) * half // ROWS)

        @pl.loop(0, tiles)
        def _(n):
            cols = pl.ds(pl.multiple_of(n * TILE, TILE), TILE)
            hgrad[n, :, span] += jnp.dot(w_v[last, cols, :], grad_t[last, :, span], preferred_element_type=f32)

            @pl.loop(part_no * half // ROWS, (part_no + 1) * half // ROWS)
            def _(r):
                rows = pl.ds(pl.multiple_of(r * ROWS, ROWS), ROWS)
                h = hgrad[n, :, rows]
                hid_tile[:, rows] = (h * upslope[n, :, rows]).astype(bf16)
                up_tile[:, rows] = (h * act[n, :, rows]).astype(bf16)

            acc_a[:, span] += jnp.dot(pgate_v[:, cols], hid_tile[:, span], preferred_element_type=f32)
            acc_b[:, span] += jnp.dot(pup_v[:, cols], up_tile[:, span], preferred_element_type=f32)

    part = jnp.concatenate([acc_a[...], acc_b[...]], axis=0).T
    high = part.astype(bf16)
    low = (part - high.astype(f32)).astype(bf16)

    @pl.loop(0, nmp)
    def _(p):
        one = jnp.dot(weighted[p], high, preferred_element_type=f32) + jnp.dot(
            weighted[p], low, preferred_element_type=f32
        )
        raw_own[p] = one
        raw_send[p] = one.astype(bf16)

    raw_copies = exchange(lambda peer: raw_send.at[peer], raw_recv, raw_ss, raw_rs)
    for copy in raw_copies:
        copy.start()
    all_sent(2)
    all_sent(3)
    for copy in fac_copies + full_copies:
        copy.wait_send()
    for copy in raw_copies:
        copy.wait_recv()
    raw = raw_own[me]
    for k in range(nmp - 1):
        raw = raw + raw_recv[k].astype(f32)

    raw_down = raw_down_v[...]

    sq_pair = jnp.sum(raw * raw, axis=0, keepdims=True)
    sq_down = jnp.sum(raw_down * raw_down, axis=0, keepdims=True)
    sq_mine[...] = jnp.concatenate(
        [sq_pair, jnp.concatenate([sq_down, jnp.zeros_like(sq_down)], axis=1), jnp.zeros((6, 2 * rank), f32)], axis=0
    )
    sq_copies = exchange(lambda peer: sq_mine, sq_recv, sq_ss, sq_rs)
    for copy in sq_copies:
        copy.start()
    for copy in sq_copies:
        copy.wait_recv()
    total = sq_mine[...]
    for k in range(nmp - 1):
        total = total + sq_recv[k]
    sq_group[...] = total
    dp_copies = [
        pltpu.make_async_remote_copy(
            src_ref=sq_group, dst_ref=sq_dp.at[k], send_sem=dp_ss.at[k], recv_sem=dp_rs.at[k],
            device_id=(peer, me), device_id_type=MESH,
        )
        for k, peer in enumerate(dp_peers)
    ]
    for copy in dp_copies:
        copy.start()
    for copy in dp_copies:
        copy.wait_recv()
    for k in range(ndp - 1):
        total = total + sq_dp[k]
    entries = seqs * ndp * rank * rank

    def scale(values):
        return lax.rsqrt(jnp.sum(values, axis=1, keepdims=True) / entries + 1e-06)

    scale_gate = scale(total[0:1, :rank])
    scale_up = scale(total[0:1, rank:])
    scale_down = scale(total[1:2, :])
    for q in range(own // 2):
        lanes = slice(q * 2 * rank, (q + 1) * 2 * rank)
        even = slice(2 * q * seqs, (2 * q + 1) * seqs)
        odd = slice((2 * q + 1) * seqs, (2 * q + 2) * seqs)
        out_ref[0, :, lanes] = jnp.concatenate([raw[even, :rank], raw[odd, :rank]], axis=1) * scale_gate
        out_ref[1, :, lanes] = jnp.concatenate([raw[even, rank:], raw[odd, rank:]], axis=1) * scale_up
        out_ref[2, :, lanes] = jnp.concatenate([raw_down[even], raw_down[odd]], axis=1) * scale_down

    for copy in raw_copies + sq_copies + dp_copies:
        copy.wait_send()


def fused_device(ndp, nmp, *args):
    layer_input, gate_pre, up_pre, out_grad, w_down, *projections, proj_output, seq_ids = args
    tokens, width = out_grad.shape
    units = w_down.shape[0]
    proj_input, proj_hidden, proj_gate, proj_upward = [proj.T for proj in projections]
    rank = proj_output.shape[0]
    own = rank // nmp
    tiles = units // TILE
    f32, bf16 = jnp.float32, jnp.bfloat16
    vmem, dma = pltpu.VMEM, pltpu.SemaphoreType.DMA
    peers, dpeers = nmp - 1, max(ndp - 1, 1)
    any_spec = pl.BlockSpec(memory_space=pl.ANY)
    result = pl.pallas_call(
        functools.partial(fused_kernel, ndp, nmp),
        out_shape=jax.ShapeDtypeStruct((3, SEQ_DEV, own * rank), f32),
        in_specs=[any_spec] * len(args),
        out_specs=pl.BlockSpec(memory_space=pltpu.VMEM),
        scratch_shapes=[
            vmem(layer_input.shape, bf16),
            vmem(gate_pre.shape, bf16),
            vmem(up_pre.shape, bf16),
            vmem((nmp, tokens, width), bf16),
            vmem((nmp, units, width), bf16),
            vmem(proj_input.shape, bf16),
            vmem((rank, units), bf16),
            vmem((rank, units), bf16),
            vmem((rank, units), bf16),
            vmem(proj_output.shape, bf16),
            vmem(seq_ids.shape, jnp.int32),
            vmem((nmp, width, tokens), bf16),
            vmem((tiles, TILE, tokens), f32),
            vmem((tiles, TILE, tokens), f32),
            vmem((tiles, TILE, tokens), f32),
            vmem((TILE, tokens), bf16),
            vmem((TILE, tokens), bf16),
            vmem((rank, tokens), f32),
            vmem((rank, tokens), f32),
            vmem((rank, tokens), f32),
            vmem((nmp, own, tokens), f32),
            vmem((peers, own, tokens), f32),
            vmem((nmp, 2 * own, tokens), bf16),
            vmem((peers, 2 * own, tokens), bf16),
            vmem((own, tokens), f32),
            vmem((own * SEQ_DEV, rank), f32),
            vmem((nmp, 2 * own, tokens), bf16),
            vmem((nmp, own * SEQ_DEV, tokens), bf16),
            vmem((nmp, own * SEQ_DEV, 2 * rank), f32),
            vmem((nmp, own * SEQ_DEV, 2 * rank), bf16),
            vmem((peers, own * SEQ_DEV, 2 * rank), bf16),
            vmem((8, 2 * rank), f32),
            vmem((peers, 8, 2 * rank), f32),
            vmem((8, 2 * rank), f32),
            vmem((dpeers, 8, 2 * rank), f32),
            dma((10,)),
            dma((nmp,)),
            dma((3, nmp)),
            dma((nmp, PIECES)),
            dma((peers,)), dma((peers,)),
            dma((peers,)), dma((peers,)),
            dma((peers,)), dma((peers,)),
            dma((peers,)), dma((peers,)),
            dma((peers,)), dma((peers,)),
            dma((dpeers,)), dma((dpeers,)),
        ],
        compiler_params=pltpu.CompilerParams(
            collective_id=0, has_side_effects=True, vmem_limit_bytes=56 * 1024 * 1024
        ),
        cost_estimate=pl.CostEstimate(
            flops=2 * tokens * units * width * nmp, bytes_accessed=2 * units * width * nmp,
            transcendentals=tokens * units,
        ),
    )(
        layer_input, gate_pre, up_pre, out_grad, w_down, proj_input, proj_hidden, proj_gate, proj_upward, proj_output,
        seq_ids,
    )
    return jnp.transpose(result, (1, 0, 2))


def solution(mesh):
    fits = mesh.shape["mp"] == ROWS_Z * COLS_X
    body = functools.partial(fused_device, mesh.shape["dp"], mesh.shape["mp"]) if fits else per_device
    in_specs = (
        P("dp", "mp"),
        P("dp", "mp"),
        P("dp", "mp"),
        P("dp", "mp"),
        P("mp", None),
        P("mp", None),
        P("mp", None),
        P("mp", None),
        P("mp", None),
        P(None, "mp"),
        P("dp", None),
    )
    out_specs = P("dp", None, "mp")
    return jax.shard_map(
        body, mesh=mesh, in_specs=in_specs, out_specs=out_specs, check_vma=False
    )
```

```python
import functools

import jax
import jax.numpy as jnp
from jax import lax
from jax.experimental import pallas as pl
from jax.experimental.pallas import tpu as pltpu
from jax.sharding import PartitionSpec as P

SEQ_DEV = 8


def silu_parts(gate_value):
    sigmoid_v = jax.nn.sigmoid(gate_value)
    return (gate_value * sigmoid_v, sigmoid_v * (1.0 + gate_value * (1.0 - sigmoid_v)))


def layer_features(member, left_in, left_hid, gate_factor, up_factor, out_factor):
    seq_count = member.shape[0]
    tok_rows = member.shape[1]
    left_width = left_in.shape[1]
    rank_dim = out_factor.shape[1]
    weighted_in = (member[:, None, :] * left_in.T[None, :, :]).reshape(
        seq_count * left_width, tok_rows
    )
    weighted_hid = (member[:, None, :] * left_hid.T[None, :, :]).reshape(
        seq_count * left_width, tok_rows
    )
    paired = jnp.dot(
        weighted_in,
        jnp.concatenate([gate_factor, up_factor], axis=1),
        precision=lax.Precision.HIGHEST,
    )
    paired = paired.reshape(seq_count, left_width, 2, rank_dim)
    gate_feat = paired[:, :, 0, :].reshape(seq_count, left_width * rank_dim)
    up_feat = paired[:, :, 1, :].reshape(seq_count, left_width * rank_dim)
    down_feat = jnp.dot(weighted_hid, out_factor, precision=lax.Precision.HIGHEST).reshape(
        seq_count, left_width * rank_dim
    )
    return jnp.stack([gate_feat, up_feat, down_feat], axis=1)


def per_device(
    layer_input,
    gate_pre,
    up_pre,
    out_grad,
    w_down,
    proj_input,
    proj_hidden,
    proj_gate,
    proj_upward,
    proj_output,
    seq_ids,
):
    contract = (((1,), (1,)), ((), ()))
    rank_dim = proj_input.shape[1]
    own_width = rank_dim // lax.axis_size("mp")
    position = lax.axis_index("mp")
    gate_value = gate_pre.astype(jnp.float32)
    up_value = up_pre.astype(jnp.float32)
    activated, slope_value = silu_parts(gate_value)
    hidden = (activated * up_value).astype(jnp.bfloat16)
    in_part = jnp.dot(layer_input, proj_input, preferred_element_type=jnp.float32)
    hid_part = jnp.dot(hidden, proj_hidden, preferred_element_type=jnp.float32)
    hidden_grad = lax.dot_general(
        lax.all_gather(out_grad, "mp", axis=1, tiled=True),
        w_down,
        contract,
        preferred_element_type=jnp.float32,
    )
    out_part = lax.dot_general(out_grad, proj_output, contract, preferred_element_type=jnp.float32)
    gate_grad = (hidden_grad * up_value * slope_value).astype(jnp.bfloat16)
    upward_grad = (hidden_grad * activated).astype(jnp.bfloat16)
    gate_part = jnp.dot(gate_grad, proj_gate, preferred_element_type=jnp.float32)
    up_part = jnp.dot(upward_grad, proj_upward, preferred_element_type=jnp.float32)
    gate_part, up_part = (gate_part, up_part)
    in_factor, hid_factor, gate_factor, up_factor, out_factor = lax.psum(
        (in_part, hid_part, gate_part, up_part, out_part), "mp"
    )
    member = (seq_ids[0][None, :] == jnp.arange(SEQ_DEV, dtype=jnp.int32)[:, None]).astype(
        jnp.float32
    )
    own_in = lax.dynamic_slice_in_dim(in_factor, position * own_width, own_width, 1)
    own_hid = lax.dynamic_slice_in_dim(hid_factor, position * own_width, own_width, 1)
    raw_feat = layer_features(member, own_in, own_hid, gate_factor, up_factor, out_factor)
    squares = jnp.sum(raw_feat * raw_feat, axis=(0, 2))
    total_sq = lax.psum(squares, ("dp", "mp"))
    entries = raw_feat.shape[0] * lax.axis_size("dp") * rank_dim * rank_dim
    scale_value = lax.rsqrt(total_sq / entries + 1e-06)
    return raw_feat * scale_value[None, :, None]


MESH = pl.DeviceIdType.MESH
ROWS_Z, COLS_X = 4, 2
PIECES = 8
X_FIRST = 1
TILE = 256
ROWS = 128
NT = (((1,), (1,)), ((), ()))
UP, DOWN, ACROSS = 0, 1, 2


def fused_kernel(
    ndp, nmp,
    x_hbm, gate_hbm, up_hbm, grad_hbm, w_hbm, pin_hbm, phid_hbm, pgate_hbm, pup_hbm, pout_hbm, seq_hbm,
    out_ref,
    x_v, gate_v, up_v, grad_v, w_v, pin_v, phid_v, pgate_v, pup_v, pout_v, seq_v,
    grad_t, hgrad, act, upslope, hid_tile, up_tile, acc_hid, acc_a, acc_b,
    fac_send, fac_recv, full, weighted, raw_down_v, raw_own, raw_send, raw_recv,
    sq_mine, sq_recv, sq_group, sq_dp,
    load_sem, w_sem, g_send, g_recv, fac_ss, fac_rs, full_ss, full_rs, raw_ss, raw_rs,
    sq_ss, sq_rs, dp_ss, dp_rs,
):
    dp = lax.axis_index("dp")
    me = lax.axis_index("mp")
    z, x = me // COLS_X, lax.rem(me, COLS_X)
    xo = 1 - x
    tokens, width = grad_hbm.shape
    tiles = w_hbm.shape[0] // TILE
    rank = pin_hbm.shape[0]
    own = rank // nmp
    prow = tokens // PIECES
    f32, bf16 = jnp.float32, jnp.bfloat16

    def at(zz, xx):
        return zz * COLS_X + xx

    loads = [
        pltpu.make_async_copy(src, dst, load_sem.at[i])
        for i, (src, dst) in enumerate(
            [
                (grad_hbm, grad_v.at[me]), (x_hbm, x_v), (pin_hbm, pin_v), (pout_hbm, pout_v), (seq_hbm, seq_v),
                (gate_hbm, gate_v), (up_hbm, up_v), (phid_hbm, phid_v), (pgate_hbm, pgate_v), (pup_hbm, pup_v),
            ]
        )
    ]
    for load in loads:
        load.start()
    w_loads = [
        pltpu.make_async_copy(w_hbm.at[:, pl.ds(b * width, width)], w_v.at[b], w_sem.at[b]) for b in range(nmp)
    ]
    for load in w_loads:
        load.start()

    barrier = pltpu.get_barrier_semaphore()
    mp_peers = [lax.rem(me + k, nmp) for k in range(1, nmp)]
    dp_peers = [lax.rem(dp + k, ndp) for k in range(1, ndp)]
    for peer in mp_peers:
        pl.semaphore_signal(barrier, inc=1, device_id=(dp, peer), device_id_type=MESH)
    for peer in dp_peers:
        pl.semaphore_signal(barrier, inc=1, device_id=(peer, me), device_id_type=MESH)
    loads[0].wait()
    pl.semaphore_wait(barrier, len(mp_peers) + len(dp_peers))

    def rows_of(kind, block, start, count, target):
        ref = grad_v.at[block, pl.ds(start, count), :]
        return pltpu.make_async_remote_copy(
            src_ref=ref, dst_ref=ref, send_sem=g_send.at[kind, block], recv_sem=g_recv.at[block, start // prow],
            device_id=(dp, target), device_id_type=MESH,
        )

    def piece(kind, block, c, target):
        return rows_of(kind, block, pl.multiple_of(c * prow, prow), prow, target)

    def arrived(block, c):
        piece(ACROSS, block, c, at(z, xo)).wait_recv()

    def upward(block, c):
        @pl.when(z < ROWS_Z - 1)
        def _():
            piece(UP, block, c, at(z + 1, x)).start()

    def downward(block, c):
        @pl.when(z > 0)
        def _():
            piece(DOWN, block, c, at(z - 1, x)).start()

    def across(block, c):
        piece(ACROSS, block, c, at(z, xo)).start()

    def inside(far):
        return (far >= 0) & (far < ROWS_Z)

    per_turn = max(ROWS // prow, 1)

    def turn(block, low=0, high=tokens // ROWS):
        @pl.loop(low, high)
        def _(r):
            rows = pl.ds(pl.multiple_of(r * ROWS, ROWS), ROWS)
            grad_t[block, :, rows] = grad_v[block, rows, :].T

    def pass_on(level, c):
        for sign, onward in ((1, downward), (-1, upward)):
            far = z + sign * level

            @pl.when(inside(far))
            def _():
                arrived(at(far, x), c)
                onward(at(far, x), c)

                @pl.when(c >= X_FIRST)
                def _():
                    across(at(far, x), c)

                @pl.when(lax.rem(c, per_turn) == per_turn - 1)
                def _():
                    turn(at(far, x), c // per_turn, c // per_turn + 1)

        @pl.when(c < X_FIRST)
        def _():
            if level == 1:
                block = at(z, xo)
                arrived(block, c)
                upward(block, c)
                downward(block, c)
                return
            for sign, onward in ((1, downward), (-1, upward)):
                far = z + sign * (level - 1)

                @pl.when(inside(far))
                def _():
                    arrived(at(far, xo), c)
                    onward(at(far, xo), c)

    def sent(kind, block, start, stop):
        if stop > start:
            target = {UP: at(z + 1, x), DOWN: at(z - 1, x), ACROSS: at(z, xo)}[kind]
            rows_of(kind, block, start * prow, (stop - start) * prow, target).wait_send()

    def all_sent(dist):
        for sign, kind in ((1, DOWN), (-1, UP)):
            far = z + sign * dist
            goes = z > 0 if kind == DOWN else z < ROWS_Z - 1

            @pl.when(inside(far) & goes)
            def _():
                sent(kind, at(far, x), 0, PIECES)
                sent(kind, at(far, xo), 0, X_FIRST)

            if dist > 0:
                @pl.when(inside(far))
                def _():
                    sent(ACROSS, at(far, x), X_FIRST, PIECES)
        if dist == 0:
            sent(ACROSS, me, 0, PIECES)

    def rest_of(block):
        @pl.loop(X_FIRST, PIECES)
        def _(c):
            arrived(block, c)

    def add_block(block, low, high, first=False):
        @pl.loop(low, high)
        def _(n):
            units = pl.ds(pl.multiple_of(n * TILE, TILE), TILE)
            part = jnp.dot(w_v[block, units, :], grad_t[block], preferred_element_type=f32)
            if first:
                hgrad[n] = part
            else:
                hgrad[n] += part

    def share(c):
        return c * tiles // PIECES, (c + 1) * tiles // PIECES

    last_z = jnp.where(z < ROWS_Z // 2, ROWS_Z - 1, 0)
    last = at(last_z, xo)

    def level_blocks(level, op_near, op_far):
        if level < ROWS_Z:
            for sign in (1, -1):
                far = z + sign * level

                @pl.when(inside(far))
                def _():
                    op_near(at(far, x))
        for sign in (1, -1) if level > 1 else (1,):
            far2 = z + sign * (level - 1)

            @pl.when(inside(far2) & (far2 != last_z))
            def _():
                op_far(at(far2, xo))

    def await_level(level):
        def whole(block):
            rest_of(block)
            turn(block)

        level_blocks(level, lambda block: None, whole)

    def add_level(level, low, high):
        add = lambda block: add_block(block, low, high)
        level_blocks(level, add, add)

    @pl.loop(0, PIECES)
    def _(c):
        across(me, c)
        upward(me, c)
        downward(me, c)

    for load in loads[1:]:
        load.wait()
    turn(me)
    out_t = jnp.dot(pout_v[...], grad_t[me], preferred_element_type=f32)
    for p in range(nmp):
        fac_send[p, 2 * own:3 * own, :] = out_t[p * own:(p + 1) * own, :]
    in_t = lax.dot_general(pin_v[...], x_v[...], NT, preferred_element_type=f32)
    for p in range(nmp):
        fac_send[p, 0:own, :] = in_t[p * own:(p + 1) * own, :]
    acc_hid[...] = jnp.zeros_like(acc_hid)

    @pl.loop(0, tiles)
    def _(n):
        cols = pl.ds(pl.multiple_of(n * TILE, TILE), TILE)

        @pl.when(n < PIECES)
        def _():
            pass_on(1, n)

        @pl.loop(0, tokens // ROWS)
        def _(r):
            rows = pl.ds(pl.multiple_of(r * ROWS, ROWS), ROWS)
            g = gate_v[rows, cols].T.astype(f32)
            u = up_v[rows, cols].T.astype(f32)
            sig = 1.0 / (1.0 + jnp.exp(-g))
            a = g * sig
            act[n, :, rows] = a
            upslope[n, :, rows] = u * (sig * (1.0 + g * (1.0 - sig)))
            hid_tile[:, rows] = (a * u).astype(bf16)

        acc_hid[...] += jnp.dot(phid_v[:, cols], hid_tile[...], preferred_element_type=f32)

    for p in range(nmp):
        fac_send[p, own:2 * own, :] = acc_hid[p * own:(p + 1) * own, :]

    def exchange(src_of, dst, send_sems, recv_sems):
        return [
            pltpu.make_async_remote_copy(
                src_ref=src_of(peer), dst_ref=dst.at[k], send_sem=send_sems.at[k], recv_sem=recv_sems.at[k],
                device_id=(dp, peer), device_id_type=MESH,
            )
            for k, peer in enumerate(mp_peers)
        ]

    fac_copies = exchange(lambda peer: fac_send.at[peer], fac_recv, fac_ss, fac_rs)
    for copy in fac_copies:
        copy.start()

    @pl.loop(min(tiles, PIECES), PIECES)
    def _(c):
        pass_on(1, c)

    for load in w_loads:
        load.wait()

    @pl.loop(0, PIECES)
    def _(c):
        pass_on(2, c)
        add_block(me, *share(c), first=True)

    await_level(1)

    for copy in fac_copies:
        copy.wait_recv()
    mine = fac_send[me]
    for k in range(nmp - 1):
        mine = mine + fac_recv[k]
    full[me] = jnp.concatenate([mine[0:own], mine[2 * own:3 * own]], axis=0).astype(bf16)
    hid_own = mine[own:2 * own]
    full_copies = [
        pltpu.make_async_remote_copy(
            src_ref=full.at[me], dst_ref=full.at[me], send_sem=full_ss.at[k], recv_sem=full_rs.at[k],
            device_id=(dp, peer), device_id_type=MESH,
        )
        for k, peer in enumerate(mp_peers)
    ]
    for copy in full_copies:
        copy.start()
    @pl.loop(0, PIECES // 2)
    def _(c):
        pass_on(3, c)
        add_level(1, *share(c))

    for copy in full_copies:
        copy.wait_recv()
    seqs = out_ref.shape[1]
    member = (seq_v[...] == lax.broadcasted_iota(jnp.int32, (seqs, tokens), 0)).astype(f32)

    @pl.loop(0, nmp)
    def _(p):
        block = full[p].astype(f32)
        weighted[p] = jnp.concatenate([block[i:i + 1, :] * member for i in range(own)], axis=0).astype(bf16)

    out_full = jnp.concatenate([full[p].astype(f32)[own:2 * own] for p in range(nmp)], axis=0)
    weighted_hid = jnp.concatenate([hid_own[i:i + 1, :] * member for i in range(own)], axis=0)
    hid_high = weighted_hid.astype(bf16)
    hid_low = (weighted_hid - hid_high.astype(f32)).astype(bf16)
    out_bf = out_full.astype(bf16)
    raw_down_v[...] = lax.dot_general(hid_high, out_bf, NT, preferred_element_type=f32) + lax.dot_general(
        hid_low, out_bf, NT, preferred_element_type=f32
    )

    @pl.loop(PIECES // 2, PIECES)
    def _(c):
        pass_on(3, c)
        add_level(1, *share(c))

    await_level(2)
    add_level(2, 0, tiles)
    await_level(3)
    add_level(3, 0, tiles)

    all_sent(0)
    all_sent(1)

    acc_a[...] = jnp.zeros_like(acc_a)
    acc_b[...] = jnp.zeros_like(acc_b)

    half = tokens // 2
    for part_no in range(2):
        at_end = (z == 0) | (z == ROWS_Z - 1)
        for c in range(part_no * PIECES // 2, (part_no + 1) * PIECES // 2):
            if c < X_FIRST:
                @pl.when(at_end)
                def _():
                    arrived(last, c)
            else:
                arrived(last, c)
        span = slice(part_no * half, (part_no + 1) * half)
        turn(last, part_no * half // ROWS, (part_no + 1) * half // ROWS)

        @pl.loop(0, tiles)
        def _(n):
            cols = pl.ds(pl.multiple_of(n * TILE, TILE), TILE)
            hgrad[n, :, span] += jnp.dot(w_v[last, cols, :], grad_t[last, :, span], preferred_element_type=f32)

            @pl.loop(part_no * half // ROWS, (part_no + 1) * half // ROWS)
            def _(r):
                rows = pl.ds(pl.multiple_of(r * ROWS, ROWS), ROWS)
                h = hgrad[n, :, rows]
                hid_tile[:, rows] = (h * upslope[n, :, rows]).astype(bf16)
                up_tile[:, rows] = (h * act[n, :, rows]).astype(bf16)

            acc_a[:, span] += jnp.dot(pgate_v[:, cols], hid_tile[:, span], preferred_element_type=f32)
            acc_b[:, span] += jnp.dot(pup_v[:, cols], up_tile[:, span], preferred_element_type=f32)

    part = jnp.concatenate([acc_a[...], acc_b[...]], axis=0).T
    high = part.astype(bf16)
    low = (part - high.astype(f32)).astype(bf16)

    @pl.loop(0, nmp)
    def _(p):
        one = jnp.dot(weighted[p], high, preferred_element_type=f32) + jnp.dot(
            weighted[p], low, preferred_element_type=f32
        )
        raw_own[p] = one
        raw_send[p] = one.astype(bf16)

    raw_copies = exchange(lambda peer: raw_send.at[peer], raw_recv, raw_ss, raw_rs)
    for copy in raw_copies:
        copy.start()
    all_sent(2)
    all_sent(3)
    for copy in fac_copies + full_copies:
        copy.wait_send()
    for copy in raw_copies:
        copy.wait_recv()
    raw = raw_own[me]
    for k in range(nmp - 1):
        raw = raw + raw_recv[k].astype(f32)

    raw_down = raw_down_v[...]

    sq_pair = jnp.sum(raw * raw, axis=0, keepdims=True)
    sq_down = jnp.sum(raw_down * raw_down, axis=0, keepdims=True)
    sq_mine[...] = jnp.concatenate(
        [sq_pair, jnp.concatenate([sq_down, jnp.zeros_like(sq_down)], axis=1), jnp.zeros((6, 2 * rank), f32)], axis=0
    )
    sq_copies = exchange(lambda peer: sq_mine, sq_recv, sq_ss, sq_rs)
    for copy in sq_copies:
        copy.start()
    for copy in sq_copies:
        copy.wait_recv()
    total = sq_mine[...]
    for k in range(nmp - 1):
        total = total + sq_recv[k]
    sq_group[...] = total
    dp_copies = [
        pltpu.make_async_remote_copy(
            src_ref=sq_group, dst_ref=sq_dp.at[k], send_sem=dp_ss.at[k], recv_sem=dp_rs.at[k],
            device_id=(peer, me), device_id_type=MESH,
        )
        for k, peer in enumerate(dp_peers)
    ]
    for copy in dp_copies:
        copy.start()
    for copy in dp_copies:
        copy.wait_recv()
    for k in range(ndp - 1):
        total = total + sq_dp[k]
    entries = seqs * ndp * rank * rank

    def scale(values):
        return lax.rsqrt(jnp.sum(values, axis=1, keepdims=True) / entries + 1e-06)

    scale_gate = scale(total[0:1, :rank])
    scale_up = scale(total[0:1, rank:])
    scale_down = scale(total[1:2, :])
    for q in range(own // 2):
        lanes = slice(q * 2 * rank, (q + 1) * 2 * rank)
        even = slice(2 * q * seqs, (2 * q + 1) * seqs)
        odd = slice((2 * q + 1) * seqs, (2 * q + 2) * seqs)
        out_ref[0, :, lanes] = jnp.concatenate([raw[even, :rank], raw[odd, :rank]], axis=1) * scale_gate
        out_ref[1, :, lanes] = jnp.concatenate([raw[even, rank:], raw[odd, rank:]], axis=1) * scale_up
        out_ref[2, :, lanes] = jnp.concatenate([raw_down[even], raw_down[odd]], axis=1) * scale_down

    for copy in raw_copies + sq_copies + dp_copies:
        copy.wait_send()


def fused_device(ndp, nmp, *args):
    layer_input, gate_pre, up_pre, out_grad, w_down, *projections, proj_output, seq_ids = args
    tokens, width = out_grad.shape
    units = w_down.shape[0]
    proj_input, proj_hidden, proj_gate, proj_upward = [proj.T for proj in projections]
    rank = proj_output.shape[0]
    own = rank // nmp
    tiles = units // TILE
    f32, bf16 = jnp.float32, jnp.bfloat16
    vmem, dma = pltpu.VMEM, pltpu.SemaphoreType.DMA
    peers, dpeers = nmp - 1, max(ndp - 1, 1)
    any_spec = pl.BlockSpec(memory_space=pl.ANY)
    result = pl.pallas_call(
        functools.partial(fused_kernel, ndp, nmp),
        out_shape=jax.ShapeDtypeStruct((3, SEQ_DEV, own * rank), f32),
        in_specs=[any_spec] * len(args),
        out_specs=pl.BlockSpec(memory_space=pltpu.VMEM),
        scratch_shapes=[
            vmem(layer_input.shape, bf16),
            vmem(gate_pre.shape, bf16),
            vmem(up_pre.shape, bf16),
            vmem((nmp, tokens, width), bf16),
            vmem((nmp, units, width), bf16),
            vmem(proj_input.shape, bf16),
            vmem((rank, units), bf16),
            vmem((rank, units), bf16),
            vmem((rank, units), bf16),
            vmem(proj_output.shape, bf16),
            vmem(seq_ids.shape, jnp.int32),
            vmem((nmp, width, tokens), bf16),
            vmem((tiles, TILE, tokens), f32),
            vmem((tiles, TILE, tokens), f32),
            vmem((tiles, TILE, tokens), f32),
            vmem((TILE, tokens), bf16),
            vmem((TILE, tokens), bf16),
            vmem((rank, tokens), f32),
            vmem((rank, tokens), f32),
            vmem((rank, tokens), f32),
            vmem((nmp, 3 * own, tokens), f32),
            vmem((peers, 3 * own, tokens), f32),
            vmem((nmp, 2 * own, tokens), bf16),
            vmem((nmp, own * SEQ_DEV, tokens), bf16),
            vmem((own * SEQ_DEV, rank), f32),
            vmem((nmp, own * SEQ_DEV, 2 * rank), f32),
            vmem((nmp, own * SEQ_DEV, 2 * rank), bf16),
            vmem((peers, own * SEQ_DEV, 2 * rank), bf16),
            vmem((8, 2 * rank), f32),
            vmem((peers, 8, 2 * rank), f32),
            vmem((8, 2 * rank), f32),
            vmem((dpeers, 8, 2 * rank), f32),
            dma((10,)),
            dma((nmp,)),
            dma((3, nmp)),
            dma((nmp, PIECES)),
            dma((peers,)), dma((peers,)),
            dma((peers,)), dma((peers,)),
            dma((peers,)), dma((peers,)),
            dma((peers,)), dma((peers,)),
            dma((dpeers,)), dma((dpeers,)),
        ],
        compiler_params=pltpu.CompilerParams(
            collective_id=0, has_side_effects=True, vmem_limit_bytes=56 * 1024 * 1024
        ),
        cost_estimate=pl.CostEstimate(
            flops=2 * tokens * units * width * nmp, bytes_accessed=2 * units * width * nmp,
            transcendentals=tokens * units,
        ),
    )(
        layer_input, gate_pre, up_pre, out_grad, w_down, proj_input, proj_hidden, proj_gate, proj_upward, proj_output,
        seq_ids,
    )
    return jnp.transpose(result, (1, 0, 2))


def solution(mesh):
    fits = mesh.shape["mp"] == ROWS_Z * COLS_X
    body = functools.partial(fused_device, mesh.shape["dp"], mesh.shape["mp"]) if fits else per_device
    in_specs = (
        P("dp", "mp"),
        P("dp", "mp"),
        P("dp", "mp"),
        P("dp", "mp"),
        P("mp", None),
        P("mp", None),
        P("mp", None),
        P("mp", None),
        P("mp", None),
        P(None, "mp"),
        P("dp", None),
    )
    out_specs = P("dp", None, "mp")
    return jax.shard_map(
        body, mesh=mesh, in_specs=in_specs, out_specs=out_specs, check_vma=False
    )
```

```python
import functools

import jax
import jax.numpy as jnp
from jax import lax
from jax.experimental import pallas as pl
from jax.experimental.pallas import tpu as pltpu
from jax.sharding import PartitionSpec as P

SEQ_DEV = 8


def silu_parts(gate_value):
    sigmoid_v = jax.nn.sigmoid(gate_value)
    return (gate_value * sigmoid_v, sigmoid_v * (1.0 + gate_value * (1.0 - sigmoid_v)))


def layer_features(member, left_in, left_hid, gate_factor, up_factor, out_factor):
    seq_count = member.shape[0]
    tok_rows = member.shape[1]
    left_width = left_in.shape[1]
    rank_dim = out_factor.shape[1]
    weighted_in = (member[:, None, :] * left_in.T[None, :, :]).reshape(
        seq_count * left_width, tok_rows
    )
    weighted_hid = (member[:, None, :] * left_hid.T[None, :, :]).reshape(
        seq_count * left_width, tok_rows
    )
    paired = jnp.dot(
        weighted_in,
        jnp.concatenate([gate_factor, up_factor], axis=1),
        precision=lax.Precision.HIGHEST,
    )
    paired = paired.reshape(seq_count, left_width, 2, rank_dim)
    gate_feat = paired[:, :, 0, :].reshape(seq_count, left_width * rank_dim)
    up_feat = paired[:, :, 1, :].reshape(seq_count, left_width * rank_dim)
    down_feat = jnp.dot(weighted_hid, out_factor, precision=lax.Precision.HIGHEST).reshape(
        seq_count, left_width * rank_dim
    )
    return jnp.stack([gate_feat, up_feat, down_feat], axis=1)


def per_device(
    layer_input,
    gate_pre,
    up_pre,
    out_grad,
    w_down,
    proj_input,
    proj_hidden,
    proj_gate,
    proj_upward,
    proj_output,
    seq_ids,
):
    contract = (((1,), (1,)), ((), ()))
    rank_dim = proj_input.shape[1]
    own_width = rank_dim // lax.axis_size("mp")
    position = lax.axis_index("mp")
    gate_value = gate_pre.astype(jnp.float32)
    up_value = up_pre.astype(jnp.float32)
    activated, slope_value = silu_parts(gate_value)
    hidden = (activated * up_value).astype(jnp.bfloat16)
    in_part = jnp.dot(layer_input, proj_input, preferred_element_type=jnp.float32)
    hid_part = jnp.dot(hidden, proj_hidden, preferred_element_type=jnp.float32)
    hidden_grad = lax.dot_general(
        lax.all_gather(out_grad, "mp", axis=1, tiled=True),
        w_down,
        contract,
        preferred_element_type=jnp.float32,
    )
    out_part = lax.dot_general(out_grad, proj_output, contract, preferred_element_type=jnp.float32)
    gate_grad = (hidden_grad * up_value * slope_value).astype(jnp.bfloat16)
    upward_grad = (hidden_grad * activated).astype(jnp.bfloat16)
    gate_part = jnp.dot(gate_grad, proj_gate, preferred_element_type=jnp.float32)
    up_part = jnp.dot(upward_grad, proj_upward, preferred_element_type=jnp.float32)
    gate_part, up_part = (gate_part, up_part)
    in_factor, hid_factor, gate_factor, up_factor, out_factor = lax.psum(
        (in_part, hid_part, gate_part, up_part, out_part), "mp"
    )
    member = (seq_ids[0][None, :] == jnp.arange(SEQ_DEV, dtype=jnp.int32)[:, None]).astype(
        jnp.float32
    )
    own_in = lax.dynamic_slice_in_dim(in_factor, position * own_width, own_width, 1)
    own_hid = lax.dynamic_slice_in_dim(hid_factor, position * own_width, own_width, 1)
    raw_feat = layer_features(member, own_in, own_hid, gate_factor, up_factor, out_factor)
    squares = jnp.sum(raw_feat * raw_feat, axis=(0, 2))
    total_sq = lax.psum(squares, ("dp", "mp"))
    entries = raw_feat.shape[0] * lax.axis_size("dp") * rank_dim * rank_dim
    scale_value = lax.rsqrt(total_sq / entries + 1e-06)
    return raw_feat * scale_value[None, :, None]


MESH = pl.DeviceIdType.MESH
ROWS_Z, COLS_X = 4, 2
PIECES = 8
X_FIRST = 1
TILE = 896
UNITS = 128
ROWS = 128
NT = (((1,), (1,)), ((), ()))
UP, DOWN, ACROSS = 0, 1, 2


def fused_kernel(
    ndp, nmp,
    x_hbm, gate_hbm, up_hbm, grad_hbm, w_hbm, pin_hbm, phid_hbm, pgate_hbm, pup_hbm, pout_hbm, seq_hbm,
    out_ref,
    x_v, gate_v, up_v, grad_v, w_v, pin_v, phid_v, pgate_v, pup_v, pout_v, seq_v,
    grad_t, hgrad, act, upslope, hid_tile, up_tile, acc_hid, acc_a, acc_b,
    fac_send, fac_recv, full, weighted, raw_down_v, raw_own, raw_send, raw_recv,
    sq_mine, sq_recv, sq_group, sq_dp,
    load_sem, w_sem, g_send, g_recv, fac_ss, fac_rs, full_ss, full_rs, raw_ss, raw_rs,
    sq_ss, sq_rs, dp_ss, dp_rs,
):
    dp = lax.axis_index("dp")
    me = lax.axis_index("mp")
    z, x = me // COLS_X, lax.rem(me, COLS_X)
    xo = 1 - x
    tokens, width = grad_hbm.shape
    tiles = w_hbm.shape[0] // TILE
    rank = pin_hbm.shape[0]
    own = rank // nmp
    prow = tokens // PIECES
    half = tokens // 2
    f32, bf16 = jnp.float32, jnp.bfloat16

    def at(zz, xx):
        return zz * COLS_X + xx

    loads = [
        pltpu.make_async_copy(src, dst, load_sem.at[i])
        for i, (src, dst) in enumerate(
            [
                (grad_hbm, grad_v.at[me]), (x_hbm, x_v), (pin_hbm, pin_v), (pout_hbm, pout_v), (seq_hbm, seq_v),
                (gate_hbm, gate_v), (up_hbm, up_v), (phid_hbm, phid_v), (pgate_hbm, pgate_v), (pup_hbm, pup_v),
            ]
        )
    ]
    for load in loads:
        load.start()
    w_loads = [
        pltpu.make_async_copy(w_hbm.at[:, pl.ds(b * width, width)], w_v.at[b], w_sem.at[b]) for b in range(nmp)
    ]
    for load in w_loads:
        load.start()

    barrier = pltpu.get_barrier_semaphore()
    mp_peers = [lax.rem(me + k, nmp) for k in range(1, nmp)]
    dp_peers = [lax.rem(dp + k, ndp) for k in range(1, ndp)]
    for peer in mp_peers:
        pl.semaphore_signal(barrier, inc=1, device_id=(dp, peer), device_id_type=MESH)
    for peer in dp_peers:
        pl.semaphore_signal(barrier, inc=1, device_id=(peer, me), device_id_type=MESH)
    loads[0].wait()
    pl.semaphore_wait(barrier, len(mp_peers) + len(dp_peers))

    def rows_of(kind, block, start, count, target):
        ref = grad_v.at[block, pl.ds(start, count), :]
        return pltpu.make_async_remote_copy(
            src_ref=ref, dst_ref=ref, send_sem=g_send.at[kind, block], recv_sem=g_recv.at[block, start // prow],
            device_id=(dp, target), device_id_type=MESH,
        )

    def piece(kind, block, c, target):
        return rows_of(kind, block, pl.multiple_of(c * prow, prow), prow, target)

    def arrived(block, c):
        piece(ACROSS, block, c, at(z, xo)).wait_recv()

    def upward(block, c):
        @pl.when(z < ROWS_Z - 1)
        def _():
            piece(UP, block, c, at(z + 1, x)).start()

    def downward(block, c):
        @pl.when(z > 0)
        def _():
            piece(DOWN, block, c, at(z - 1, x)).start()

    def across(block, c):
        piece(ACROSS, block, c, at(z, xo)).start()

    def inside(far):
        return (far >= 0) & (far < ROWS_Z)

    per_turn = max(ROWS // prow, 1)

    def turn(block, low=0, high=tokens // ROWS):
        @pl.loop(low, high)
        def _(r):
            rows = pl.ds(pl.multiple_of(r * ROWS, ROWS), ROWS)
            grad_t[block, :, rows] = grad_v[block, rows, :].T

    def pass_on(level, c):
        for sign, onward in ((1, downward), (-1, upward)):
            far = z + sign * level

            @pl.when(inside(far))
            def _():
                arrived(at(far, x), c)
                onward(at(far, x), c)

                @pl.when(c >= X_FIRST)
                def _():
                    across(at(far, x), c)

                @pl.when(lax.rem(c, per_turn) == per_turn - 1)
                def _():
                    turn(at(far, x), c // per_turn, c // per_turn + 1)

        @pl.when(c < X_FIRST)
        def _():
            if level == 1:
                block = at(z, xo)
                arrived(block, c)
                upward(block, c)
                downward(block, c)
                return
            for sign, onward in ((1, downward), (-1, upward)):
                far = z + sign * (level - 1)

                @pl.when(inside(far))
                def _():
                    arrived(at(far, xo), c)
                    onward(at(far, xo), c)

    def sent(kind, block, start, stop):
        if stop > start:
            target = {UP: at(z + 1, x), DOWN: at(z - 1, x), ACROSS: at(z, xo)}[kind]
            rows_of(kind, block, start * prow, (stop - start) * prow, target).wait_send()

    def all_sent(dist):
        for sign, kind in ((1, DOWN), (-1, UP)):
            far = z + sign * dist
            goes = z > 0 if kind == DOWN else z < ROWS_Z - 1

            @pl.when(inside(far) & goes)
            def _():
                sent(kind, at(far, x), 0, PIECES)
                sent(kind, at(far, xo), 0, X_FIRST)

            if dist > 0:
                @pl.when(inside(far))
                def _():
                    sent(ACROSS, at(far, x), X_FIRST, PIECES)
        if dist == 0:
            sent(ACROSS, me, 0, PIECES)

    def rest_of(block):
        @pl.loop(X_FIRST, PIECES)
        def _(c):
            arrived(block, c)

    def add_block(block, low, high, first=False):
        @pl.loop(low, high)
        def _(n):
            units = pl.ds(pl.multiple_of(n * TILE, TILE), TILE)
            part = jnp.dot(w_v[block, units, :], grad_t[block], preferred_element_type=f32)
            if first:
                hgrad[n] = part
            else:
                hgrad[n] += part

    def share(c):
        return c * tiles // PIECES, (c + 1) * tiles // PIECES

    last_z = jnp.where(z < ROWS_Z // 2, ROWS_Z - 1, 0)
    last = at(last_z, xo)

    def level_blocks(level, op_near, op_far):
        if level < ROWS_Z:
            for sign in (1, -1):
                far = z + sign * level

                @pl.when(inside(far))
                def _():
                    op_near(at(far, x))
        for sign in (1, -1) if level > 1 else (1,):
            far2 = z + sign * (level - 1)

            @pl.when(inside(far2) & (far2 != last_z))
            def _():
                op_far(at(far2, xo))

    def await_level(level):
        def whole(block):
            rest_of(block)
            turn(block)

        level_blocks(level, lambda block: None, whole)

    def add_level(level, low, high):
        add = lambda block: add_block(block, low, high)
        level_blocks(level, add, add)

    @pl.loop(0, PIECES)
    def _(c):
        across(me, c)
        upward(me, c)
        downward(me, c)

    for load in loads[1:]:
        load.wait()
    turn(me)
    out_t = jnp.dot(pout_v[...], grad_t[me], preferred_element_type=f32)
    for p in range(nmp):
        fac_send[p, 2 * own:3 * own, :] = out_t[p * own:(p + 1) * own, :]
    in_t = lax.dot_general(pin_v[...], x_v[...], NT, preferred_element_type=f32)
    for p in range(nmp):
        fac_send[p, 0:own, :] = in_t[p * own:(p + 1) * own, :]
    acc_hid[...] = jnp.zeros_like(acc_hid)

    @pl.loop(0, tiles)
    def _(n):
        cols = pl.ds(pl.multiple_of(n * TILE, TILE), TILE)

        @pl.loop(0, TILE // UNITS)
        def _(k):
            for r in range(tokens // half):
                rows = slice(r * half, (r + 1) * half)
                units = pl.ds(pl.multiple_of(k * UNITS, UNITS), UNITS)
                lanes = pl.ds(pl.multiple_of(n * TILE + k * UNITS, UNITS), UNITS)
                g = gate_v[rows, lanes].T.astype(f32)
                u = up_v[rows, lanes].T.astype(f32)
                sig = 1.0 / (1.0 + jnp.exp(-g))
                a = g * sig
                act[n, units, rows] = a
                upslope[n, units, rows] = u * (sig * (1.0 + g * (1.0 - sig)))
                hid_tile[units, rows] = (a * u).astype(bf16)

        acc_hid[...] += jnp.dot(phid_v[:, cols], hid_tile[...], preferred_element_type=f32)

    for p in range(nmp):
        fac_send[p, own:2 * own, :] = acc_hid[p * own:(p + 1) * own, :]

    def exchange(src_of, dst, send_sems, recv_sems):
        return [
            pltpu.make_async_remote_copy(
                src_ref=src_of(peer), dst_ref=dst.at[k], send_sem=send_sems.at[k], recv_sem=recv_sems.at[k],
                device_id=(dp, peer), device_id_type=MESH,
            )
            for k, peer in enumerate(mp_peers)
        ]

    fac_copies = exchange(lambda peer: fac_send.at[peer], fac_recv, fac_ss, fac_rs)
    for copy in fac_copies:
        copy.start()

    for load in w_loads:
        load.wait()

    @pl.loop(0, PIECES)
    def _(c):
        pass_on(1, c)
        add_block(me, *share(c), first=True)

    await_level(1)

    @pl.loop(0, PIECES)
    def _(c):
        pass_on(2, c)
        add_level(1, *share(c))

    for copy in fac_copies:
        copy.wait_recv()
    mine = fac_send[me]
    for k in range(nmp - 1):
        mine = mine + fac_recv[k]
    full[me] = jnp.concatenate([mine[0:own], mine[2 * own:3 * own]], axis=0).astype(bf16)
    hid_own = mine[own:2 * own]
    full_copies = [
        pltpu.make_async_remote_copy(
            src_ref=full.at[me], dst_ref=full.at[me], send_sem=full_ss.at[k], recv_sem=full_rs.at[k],
            device_id=(dp, peer), device_id_type=MESH,
        )
        for k, peer in enumerate(mp_peers)
    ]
    for copy in full_copies:
        copy.start()
    await_level(2)

    @pl.loop(0, PIECES // 2)
    def _(c):
        pass_on(3, c)
        add_level(2, *share(c))

    for copy in full_copies:
        copy.wait_recv()
    seqs = out_ref.shape[1]
    member = (seq_v[...] == lax.broadcasted_iota(jnp.int32, (seqs, tokens), 0)).astype(f32)

    @pl.loop(0, nmp)
    def _(p):
        block = full[p].astype(f32)
        weighted[p] = jnp.concatenate([block[i:i + 1, :] * member for i in range(own)], axis=0).astype(bf16)

    out_full = jnp.concatenate([full[p].astype(f32)[own:2 * own] for p in range(nmp)], axis=0)
    weighted_hid = jnp.concatenate([hid_own[i:i + 1, :] * member for i in range(own)], axis=0)
    hid_high = weighted_hid.astype(bf16)
    hid_low = (weighted_hid - hid_high.astype(f32)).astype(bf16)
    out_bf = out_full.astype(bf16)
    raw_down_v[...] = lax.dot_general(hid_high, out_bf, NT, preferred_element_type=f32) + lax.dot_general(
        hid_low, out_bf, NT, preferred_element_type=f32
    )

    @pl.loop(PIECES // 2, PIECES)
    def _(c):
        pass_on(3, c)
        add_level(2, *share(c))

    await_level(3)
    add_level(3, 0, tiles)

    all_sent(0)
    all_sent(1)

    acc_a[...] = jnp.zeros_like(acc_a)
    acc_b[...] = jnp.zeros_like(acc_b)

    for part_no in range(2):
        at_end = (z == 0) | (z == ROWS_Z - 1)
        for c in range(part_no * PIECES // 2, (part_no + 1) * PIECES // 2):
            if c < X_FIRST:
                @pl.when(at_end)
                def _():
                    arrived(last, c)
            else:
                arrived(last, c)
        span = slice(part_no * half, (part_no + 1) * half)
        turn(last, part_no * half // ROWS, (part_no + 1) * half // ROWS)

        @pl.loop(0, tiles)
        def _(n):
            cols = pl.ds(pl.multiple_of(n * TILE, TILE), TILE)
            hgrad[n, :, span] += jnp.dot(w_v[last, cols, :], grad_t[last, :, span], preferred_element_type=f32)

            @pl.loop(0, TILE // UNITS)
            def _(k):
                units = pl.ds(pl.multiple_of(k * UNITS, UNITS), UNITS)
                h = hgrad[n, units, span]
                hid_tile[units, span] = (h * upslope[n, units, span]).astype(bf16)
                up_tile[units, span] = (h * act[n, units, span]).astype(bf16)

            acc_a[:, span] += jnp.dot(pgate_v[:, cols], hid_tile[:, span], preferred_element_type=f32)
            acc_b[:, span] += jnp.dot(pup_v[:, cols], up_tile[:, span], preferred_element_type=f32)

    part = jnp.concatenate([acc_a[...], acc_b[...]], axis=0).T
    high = part.astype(bf16)
    low = (part - high.astype(f32)).astype(bf16)

    @pl.loop(0, nmp)
    def _(p):
        one = jnp.dot(weighted[p], high, preferred_element_type=f32) + jnp.dot(
            weighted[p], low, preferred_element_type=f32
        )
        raw_own[p] = one
        raw_send[p] = one.astype(bf16)

    raw_copies = exchange(lambda peer: raw_send.at[peer], raw_recv, raw_ss, raw_rs)
    for copy in raw_copies:
        copy.start()
    all_sent(2)
    all_sent(3)
    for copy in fac_copies + full_copies:
        copy.wait_send()
    for copy in raw_copies:
        copy.wait_recv()
    raw = raw_own[me]
    for k in range(nmp - 1):
        raw = raw + raw_recv[k].astype(f32)

    raw_down = raw_down_v[...]

    sq_pair = jnp.sum(raw * raw, axis=0, keepdims=True)
    sq_down = jnp.sum(raw_down * raw_down, axis=0, keepdims=True)
    sq_mine[...] = jnp.concatenate(
        [sq_pair, jnp.concatenate([sq_down, jnp.zeros_like(sq_down)], axis=1), jnp.zeros((6, 2 * rank), f32)], axis=0
    )
    sq_copies = exchange(lambda peer: sq_mine, sq_recv, sq_ss, sq_rs)
    for copy in sq_copies:
        copy.start()
    for copy in sq_copies:
        copy.wait_recv()
    total = sq_mine[...]
    for k in range(nmp - 1):
        total = total + sq_recv[k]
    sq_group[...] = total
    dp_copies = [
        pltpu.make_async_remote_copy(
            src_ref=sq_group, dst_ref=sq_dp.at[k], send_sem=dp_ss.at[k], recv_sem=dp_rs.at[k],
            device_id=(peer, me), device_id_type=MESH,
        )
        for k, peer in enumerate(dp_peers)
    ]
    for copy in dp_copies:
        copy.start()
    for copy in dp_copies:
        copy.wait_recv()
    for k in range(ndp - 1):
        total = total + sq_dp[k]
    entries = seqs * ndp * rank * rank

    def scale(values):
        return lax.rsqrt(jnp.sum(values, axis=1, keepdims=True) / entries + 1e-06)

    scale_gate = scale(total[0:1, :rank])
    scale_up = scale(total[0:1, rank:])
    scale_down = scale(total[1:2, :])
    for q in range(own // 2):
        lanes = slice(q * 2 * rank, (q + 1) * 2 * rank)
        even = slice(2 * q * seqs, (2 * q + 1) * seqs)
        odd = slice((2 * q + 1) * seqs, (2 * q + 2) * seqs)
        out_ref[0, :, lanes] = jnp.concatenate([raw[even, :rank], raw[odd, :rank]], axis=1) * scale_gate
        out_ref[1, :, lanes] = jnp.concatenate([raw[even, rank:], raw[odd, rank:]], axis=1) * scale_up
        out_ref[2, :, lanes] = jnp.concatenate([raw_down[even], raw_down[odd]], axis=1) * scale_down

    for copy in raw_copies + sq_copies + dp_copies:
        copy.wait_send()


def fused_device(ndp, nmp, *args):
    layer_input, gate_pre, up_pre, out_grad, w_down, *projections, proj_output, seq_ids = args
    tokens, width = out_grad.shape
    units = w_down.shape[0]
    proj_input, proj_hidden, proj_gate, proj_upward = [proj.T for proj in projections]
    rank = proj_output.shape[0]
    own = rank // nmp
    tiles = units // TILE
    f32, bf16 = jnp.float32, jnp.bfloat16
    vmem, dma = pltpu.VMEM, pltpu.SemaphoreType.DMA
    peers, dpeers = nmp - 1, max(ndp - 1, 1)
    any_spec = pl.BlockSpec(memory_space=pl.ANY)
    result = pl.pallas_call(
        functools.partial(fused_kernel, ndp, nmp),
        out_shape=jax.ShapeDtypeStruct((3, SEQ_DEV, own * rank), f32),
        in_specs=[any_spec] * len(args),
        out_specs=pl.BlockSpec(memory_space=pltpu.VMEM),
        scratch_shapes=[
            vmem(layer_input.shape, bf16),
            vmem(gate_pre.shape, bf16),
            vmem(up_pre.shape, bf16),
            vmem((nmp, tokens, width), bf16),
            vmem((nmp, units, width), bf16),
            vmem(proj_input.shape, bf16),
            vmem((rank, units), bf16),
            vmem((rank, units), bf16),
            vmem((rank, units), bf16),
            vmem(proj_output.shape, bf16),
            vmem(seq_ids.shape, jnp.int32),
            vmem((nmp, width, tokens), bf16),
            vmem((tiles, TILE, tokens), f32),
            vmem((tiles, TILE, tokens), f32),
            vmem((tiles, TILE, tokens), f32),
            vmem((TILE, tokens), bf16),
            vmem((TILE, tokens), bf16),
            vmem((rank, tokens), f32),
            vmem((rank, tokens), f32),
            vmem((rank, tokens), f32),
            vmem((nmp, 3 * own, tokens), f32),
            vmem((peers, 3 * own, tokens), f32),
            vmem((nmp, 2 * own, tokens), bf16),
            vmem((nmp, own * SEQ_DEV, tokens), bf16),
            vmem((own * SEQ_DEV, rank), f32),
            vmem((nmp, own * SEQ_DEV, 2 * rank), f32),
            vmem((nmp, own * SEQ_DEV, 2 * rank), bf16),
            vmem((peers, own * SEQ_DEV, 2 * rank), bf16),
            vmem((8, 2 * rank), f32),
            vmem((peers, 8, 2 * rank), f32),
            vmem((8, 2 * rank), f32),
            vmem((dpeers, 8, 2 * rank), f32),
            dma((10,)),
            dma((nmp,)),
            dma((3, nmp)),
            dma((nmp, PIECES)),
            dma((peers,)), dma((peers,)),
            dma((peers,)), dma((peers,)),
            dma((peers,)), dma((peers,)),
            dma((peers,)), dma((peers,)),
            dma((dpeers,)), dma((dpeers,)),
        ],
        compiler_params=pltpu.CompilerParams(
            collective_id=0, has_side_effects=True, vmem_limit_bytes=56 * 1024 * 1024
        ),
        cost_estimate=pl.CostEstimate(
            flops=2 * tokens * units * width * nmp, bytes_accessed=2 * units * width * nmp,
            transcendentals=tokens * units,
        ),
    )(
        layer_input, gate_pre, up_pre, out_grad, w_down, proj_input, proj_hidden, proj_gate, proj_upward, proj_output,
        seq_ids,
    )
    return jnp.transpose(result, (1, 0, 2))


def solution(mesh):
    fits = mesh.shape["mp"] == ROWS_Z * COLS_X
    body = functools.partial(fused_device, mesh.shape["dp"], mesh.shape["mp"]) if fits else per_device
    in_specs = (
        P("dp", "mp"),
        P("dp", "mp"),
        P("dp", "mp"),
        P("dp", "mp"),
        P("mp", None),
        P("mp", None),
        P("mp", None),
        P("mp", None),
        P("mp", None),
        P(None, "mp"),
        P("dp", None),
    )
    out_specs = P("dp", None, "mp")
    return jax.shard_map(
        body, mesh=mesh, in_specs=in_specs, out_specs=out_specs, check_vma=False
    )
```
